128 devices in a mesh: row: 16 (over x, y_lo, core), col: 8 (over y_hi, z).
Axes of the slice: x: 4, y: 4 (y_hi: 2, y_lo: 2; y = y_hi * 2 + y_lo), z: 4, core: 2. Of those that a mesh axis runs over, the one named last changes fastest.
Arguments:
- front: float32 [16384, 16384], P('row', 'col'), may hold values from -0.03 to 5, as said below
- children: float32 [2, 6144, 6144], P(None, 'row', 'col'), may hold values from -0.02 to 1, as said below
- child_map: int32 [2, 48], replicated, may hold values from 0 to 127, as said below
Outputs:
- front_out: float32 [16384, 16384], P('row', 'col')
- lower_panel: float32 [16384, 1024], P('row')
The draws below stay inside these ranges and needn't reach their ends.
Inputs may be any that keep to these rules, and one draw needn't show every extreme that they name: Each row of child_map is strictly increasing; each aligned run of 16 child tiles maps to 16 consecutive parent tiles. `front`: symmetric in natural order, and the assembled front is positive definite. `children`: each block is symmetric in natural order.
All inputs are finite; a program needn't handle non-finite values.
Results may differ from the reference program's by a relative error of at most 0.0001.
Values sent between devices are 32-bit elements; how exact they have to be, the bound alone decides.
A program may use at most 128 MiB of HBM per device.

```python
import math
import jax
import jax.numpy as jnp
from jax import lax

FRONT = 16384
CHILD = 6144
TILE = 128
RUN = 16
PANEL = 512
PIVOTS = 1024
GRID_R = 16
GRID_C = 8
N_ROW = 16
N_COL = 8


front_length = 8.0


child_length = 2.5


def rows_stored_drawn(natural, grid_size):
    per_device = natural.shape[0] // (grid_size * TILE)
    shaped = natural.reshape((per_device, grid_size, TILE) + natural.shape[1:])
    return jnp.swapaxes(shaped, 0, 1).reshape(natural.shape)


def stored_order(natural):
    by_rows = rows_stored_drawn(natural, GRID_R)
    return rows_stored_drawn(by_rows.T, GRID_C).T


def kernel_matrix(key, order, coefficient, length, ordered_count):
    key_perm, key_jitter = jax.random.split(key)
    leading = jnp.arange(ordered_count, dtype=jnp.int32)
    trailing = jax.random.permutation(key_perm, order - ordered_count).astype(jnp.int32) + ordered_count
    lattice = jnp.concatenate([leading, trailing]).astype(jnp.float32)
    positions = lattice + 0.5 * jax.random.uniform(key_jitter, (order,), jnp.float32)
    return coefficient * jnp.exp(-jnp.abs(positions[:, None] - positions[None, :]) / length)


def on_diagonal(order):
    numbers = jnp.arange(order, dtype=jnp.int32)
    return numbers[:, None] == numbers[None, :]


def draw_front(key, part):
    key = jax.random.fold_in(key, 11)
    key_points, key_off, key_diag = jax.random.split(key, 3)
    sigma = 0.35 / math.sqrt(FRONT)
    noise = jax.random.uniform(key_off, (FRONT, FRONT), jnp.float32, -1.7320508 * sigma, 1.7320508 * sigma)
    diag_values = jax.random.uniform(key_diag, (FRONT,), jnp.float32, 2.5, 4.0)
    kernel = kernel_matrix(key_points, FRONT, 1.0, front_length, PIVOTS)
    mirrored = (noise + noise.T) * 0.70710678
    natural = jnp.where(on_diagonal(FRONT), kernel + diag_values[None, :], kernel + mirrored)
    return stored_order(natural)


def draw_children(key, part):
    key = jax.random.fold_in(key, 23)
    sigma = 0.2 / math.sqrt(CHILD)
    blocks = []
    for child_index in range(2):
        key_points, key_off, key_diag = jax.random.split(jax.random.fold_in(key, child_index), 3)
        noise = jax.random.uniform(key_off, (CHILD, CHILD), jnp.float32, -1.7320508 * sigma, 1.7320508 * sigma)
        diag_extra = jax.random.uniform(key_diag, (CHILD,), jnp.float32, 0.0, 0.25)
        kernel = kernel_matrix(key_points, CHILD, 0.75, child_length, 0)
        mirrored = (noise + noise.T) * 0.70710678
        natural = jnp.where(on_diagonal(CHILD), kernel + diag_extra[None, :], kernel + mirrored)
        blocks.append(stored_order(natural))
    return jnp.stack(blocks)


def draw_child_map(key, part):
    key = jax.random.fold_in(key, 37)
    run_count = CHILD // (TILE * RUN)
    slack = FRONT // TILE - CHILD // TILE
    cuts = jnp.sort(jax.random.randint(key, (2, run_count), 0, slack + 1), axis=1)
    cuts = cuts.at[0, 0].set(0).at[1, run_count - 1].set(slack)
    starts = cuts + jnp.arange(run_count, dtype=jnp.int32)[None, :] * RUN
    spread = starts[:, :, None] + jnp.arange(RUN, dtype=jnp.int32)[None, None, :]
    return spread.reshape(2, run_count * RUN).astype(jnp.int32)


def setup_inputs(seed: int = 0) -> dict:
    arg_keys = jax.random.split(jax.random.key(seed), 4)
    front = draw_front(jax.random.fold_in(arg_keys[3], 71), 0)
    children = draw_children(jax.random.fold_in(arg_keys[3], 71), 0)
    child_map = draw_child_map(jax.random.fold_in(arg_keys[3], 71), 0)
    return {"front": front, "children": children, "child_map": child_map}


HIGHEST = lax.Precision.HIGHEST

def rows_natural(stored, grid_size, tile_size):
    per_device = stored.shape[0] // (grid_size * tile_size)
    shaped = stored.reshape((grid_size, per_device, tile_size) + stored.shape[1:])
    return jnp.swapaxes(shaped, 0, 1).reshape(stored.shape)

def rows_stored(natural, grid_size, tile_size):
    per_device = natural.shape[0] // (grid_size * tile_size)
    shaped = natural.reshape((per_device, grid_size, tile_size) + natural.shape[1:])
    return jnp.swapaxes(shaped, 0, 1).reshape(natural.shape)

def both_natural(stored):
    by_rows = rows_natural(stored, N_ROW, TILE)
    return rows_natural(by_rows.T, N_COL, TILE).T

def both_stored(natural):
    by_rows = rows_stored(natural, N_ROW, TILE)
    return rows_stored(by_rows.T, N_COL, TILE).T

def reference(front, children, child_map):
    assembled = both_natural(front)
    offsets = jnp.arange(TILE, dtype=jnp.int32)
    for child_index in range(2):
        natural_child = both_natural(children[child_index])
        positions = (child_map[child_index][:, None] * TILE + offsets[None, :]).reshape(-1).astype(jnp.int32)
        assembled = assembled.at[positions[:, None], positions[None, :]].add(natural_child)
    working = assembled
    lower_natural = jnp.zeros((FRONT, PIVOTS), jnp.float32)
    for panel_index in range(PIVOTS // PANEL):
        first_col = panel_index * PANEL
        after_col = first_col + PANEL
        diagonal_factor = jnp.linalg.cholesky(working[first_col:after_col, first_col:after_col])
        below_rows = jax.scipy.linalg.solve_triangular(diagonal_factor, working[after_col:, first_col:after_col].T, lower=True).T
        lower_natural = lower_natural.at[first_col:after_col, first_col:after_col].set(diagonal_factor)
        lower_natural = lower_natural.at[after_col:, first_col:after_col].set(below_rows)
        working = working.at[after_col:, after_col:].add(-jnp.dot(below_rows, below_rows.T, precision=HIGHEST))
    front_natural = assembled.at[PIVOTS:, PIVOTS:].set(working[PIVOTS:, PIVOTS:])
    return (both_stored(front_natural), rows_stored(lower_natural, N_ROW, TILE))
```

```python
import jax
import jax.numpy as jnp
from jax import lax
from jax.experimental import pallas as pl
from jax.experimental.pallas import tpu as pltpu
from jax.sharding import PartitionSpec as P

f32 = jnp.float32
bf16 = jnp.bfloat16
TILE = 128
RUN = 16
PIVOTS = 1024
STEPS = PIVOTS // TILE
HIGH = lax.Precision.HIGH
SUB = 8
GROUPS = TILE // SUB
ITEMS = 36
SHARE = 5
MIB = 2**20


def split2(x):
    hi = x.astype(bf16)
    return hi, (x - hi.astype(f32)).astype(bf16)


def split3(x):
    hi = x.astype(bf16).astype(f32)
    rest = x - hi
    mid = rest.astype(bf16).astype(f32)
    return hi, mid, rest - mid


def mm3(a, b, dims):
    ah, al = split2(a)
    bh, bl = split2(b)

    def dot(x, y):
        return lax.dot_general(x, y, (dims, ((), ())), preferred_element_type=f32)

    return dot(ah, bh) + (dot(ah, bl) + dot(al, bh))


def lane(x, k):
    return jnp.broadcast_to(x[:, k : k + 1], (SUB, TILE))


def sublane(x, k):
    return jnp.broadcast_to(x[k : k + 1, :], (SUB, TILE))


def factor_tile(a, e):
    row_of = lax.broadcasted_iota(jnp.int32, (SUB, TILE), 0)

    def packed(v):
        out = v[SUB - 1]
        for t in range(SUB - 2, -1, -1):
            out = jnp.where(row_of == t, v[t], out)
        return out

    inverse_rows = []
    last_u = last_e = None
    for b in range(GROUPS):
        r = [sublane(a[b], t) for t in range(SUB)]
        w = [sublane(e[b], t) for t in range(SUB)]
        if b:
            for s in range(SUB):
                for t in range(SUB):
                    factor = lane(last_u[t], SUB * b + s)
                    r[s] = r[s] - factor * last_u[t]
                    w[s] = w[s] - factor * last_e[t]
        d = [[lane(r[t], SUB * b + s) if s >= t else None for t in range(SUB)] for s in range(SUB)]
        u = [None] * SUB
        v = [None] * SUB
        for t in range(SUB):
            scale = lax.rsqrt(d[t][t])
            u[t] = r[t] * scale
            v[t] = w[t] * scale
            below = [d[s][t] * scale if s > t else None for s in range(SUB)]
            for s in range(t + 1, SUB):
                for q in range(t + 1, s + 1):
                    d[s][q] = d[s][q] - below[s] * below[q]
            for s in range(t + 1, SUB):
                r[s] = r[s] - below[s] * u[t]
                w[s] = w[s] - below[s] * v[t]
        last_u, last_e = u, v
        urows, erows = packed(u), packed(v)
        inverse_rows.append(erows)
        if b < GROUPS - 2:
            uh, um, ul = split3(urows)
            eh, em, el = split3(erows)
            left = jnp.concatenate([uh, uh, um, um, uh, ul], 0).astype(bf16)
            right = jnp.concatenate(
                [jnp.concatenate([uh, um, uh, um, ul, uh], 0), jnp.concatenate([eh, em, eh, em, el, eh], 0)], 1
            ).astype(bf16)
            change = lax.dot_general(left, right, (((0,), (0,)), ((), ())), preferred_element_type=f32)
            for i in range(b + 2, GROUPS):
                a[i] = a[i] - change[SUB * i : SUB * i + SUB, :TILE]
                e[i] = e[i] - change[SUB * i : SUB * i + SUB, TILE:]
    return jnp.concatenate(inverse_rows, 0)


def factor_kernel(block_ref, inverse_ref, work):
    width = (STEPS + 1) * TILE
    for i in range(STEPS):
        rows = slice(i * TILE, (i + 1) * TILE)
        work[rows, :PIVOTS] = block_ref[rows, :]
        ri = lax.broadcasted_iota(jnp.int32, (TILE, PIVOTS), 0) + i * TILE
        ci = lax.broadcasted_iota(jnp.int32, (TILE, PIVOTS), 1)
        work[rows, PIVOTS:] = (ri == ci).astype(f32)

    @pl.loop(0, STEPS)
    def _(k):
        kb = pl.ds(pl.multiple_of(k * TILE, TILE), TILE)
        window = pl.ds(pl.multiple_of(k * TILE, TILE), width)
        tile = work[kb, kb]
        ri = lax.broadcasted_iota(jnp.int32, (SUB, TILE), 0)
        ci = lax.broadcasted_iota(jnp.int32, (SUB, TILE), 1)
        a = [tile[SUB * i : SUB * i + SUB] for i in range(GROUPS)]
        e = [(ri + SUB * i == ci).astype(f32) for i in range(GROUPS)]
        inverse = factor_tile(a, e)
        work[kb, window] = mm3(inverse, work[kb, window], ((1,), (0,)))

        @pl.loop(k + 1, STEPS)
        def _(i):
            ib = pl.ds(pl.multiple_of(i * TILE, TILE), TILE)
            work[ib, window] -= mm3(work[kb, ib], work[kb, window], ((0,), (0,)))

    inverse_ref[...] = work[:, PIVOTS:]


def inverse_factor(block):
    vmem = pl.BlockSpec(memory_space=pltpu.VMEM)
    return pl.pallas_call(
        factor_kernel,
        out_shape=jax.ShapeDtypeStruct((PIVOTS, PIVOTS), f32),
        in_specs=[vmem],
        out_specs=vmem,
        scratch_shapes=[pltpu.VMEM((PIVOTS, 2 * PIVOTS), f32)],
        compiler_params=pltpu.CompilerParams(vmem_limit_bytes=40 * MIB),
        cost_estimate=pl.CostEstimate(flops=5 * 10**10, bytes_accessed=8 * MIB, transcendentals=0),
        name="factor",
    )(block)


def reorder_kernel(index_ref, in_ref, out_ref):
    @pl.loop(0, in_ref.shape[0])
    def _(d):
        for m in range(SHARE):
            out_ref[d, m] = in_ref[index_ref[d, m], m]


def reorder(pieces, index):
    vmem = pl.BlockSpec(memory_space=pltpu.VMEM)
    return pl.pallas_call(
        reorder_kernel,
        out_shape=jax.ShapeDtypeStruct(pieces.shape, f32),
        in_specs=[pl.BlockSpec(memory_space=pltpu.SMEM), vmem],
        out_specs=vmem,
        compiler_params=pltpu.CompilerParams(vmem_limit_bytes=16 * MIB),
        name="reorder",
    )(index, pieces)


def relay(children, child_map, rows, cols, row_index, col_index):
    pieces = children.reshape(2, 3, rows, SUB, 6, TILE).transpose(2, 0, 1, 4, 3, 5).reshape(rows, ITEMS, SUB, TILE)
    pieces = jnp.pad(pieces, ((0, 0), (0, cols * SHARE - ITEMS), (0, 0), (0, 0)))
    pieces = pieces.reshape(rows * cols, SHARE, SUB, TILE)
    held = lax.all_to_all(pieces, ("row", "col"), 0, 0, tiled=True)
    item = jnp.minimum(col_index * SHARE + jnp.arange(SHARE), ITEMS - 1)
    child, run, tile = item // 18, item % 18 // 6, item % 6
    row_start = child_map[child, run * RUN]
    col_start = child_map[child, tile // 2 * RUN]
    target = jnp.arange(rows * cols, dtype=jnp.int32)[:, None]
    index = (target // cols - row_start) % rows * cols + (target % cols - col_start) % cols
    held = reorder(held, index.astype(jnp.int32))
    back = lax.all_to_all(held, ("row", "col"), 0, 0, tiled=True)
    return back.reshape(rows, cols * SHARE, SUB, TILE)[:, :ITEMS]


def assemble_kernel(slots_ref, front_ref, items_ref, out_ref):
    out_ref[...] = front_ref[...]
    for m in range(ITEMS):
        row = pl.ds(pl.multiple_of(slots_ref[0, m] * TILE, TILE), TILE)
        col = pl.ds(pl.multiple_of(slots_ref[1, m] * TILE, TILE), TILE)
        out_ref[row, col] += items_ref[:, m].reshape(TILE, TILE)


def assemble(front, items, child_map, rows, cols, row_index, col_index):
    item = jnp.arange(ITEMS)
    child, run, tile = item // 18, item % 18 // 6, item % 6
    row_start = child_map[child, run * RUN]
    col_start = child_map[child, tile // 2 * RUN]
    row_slot = (row_start + (row_index - row_start) % rows) // rows
    col_slot = (col_start + (col_index - col_start) % cols) // cols + tile % 2
    slots = jnp.stack([row_slot, col_slot]).astype(jnp.int32)
    vmem = pl.BlockSpec(memory_space=pltpu.VMEM)
    return pl.pallas_call(
        assemble_kernel,
        out_shape=jax.ShapeDtypeStruct(front.shape, f32),
        in_specs=[pl.BlockSpec(memory_space=pltpu.SMEM), vmem, vmem],
        out_specs=vmem,
        compiler_params=pltpu.CompilerParams(vmem_limit_bytes=32 * MIB),
        name="assemble",
    )(slots, front, items)


def per_device(front, children, child_map):
    rows, cols = lax.axis_size("row"), lax.axis_size("col")
    row_index, col_index = lax.axis_index("row"), lax.axis_index("col")
    local_rows, local_cols = front.shape
    items = relay(children, child_map, rows, cols, row_index, col_index)
    assembled = assemble(front, items, child_map, rows, cols, row_index, col_index)
    row_strip = assembled[:, :TILE]
    col_strip = assembled[:TILE, :]
    half = TILE // 2
    upper = row_index < STEPS
    route = [(i, i + STEPS) for i in range(STEPS)] + [(i + STEPS, i) for i in range(STEPS)]
    second = lax.ppermute(col_strip[half:], "row", route)
    shared = jnp.where(upper, col_strip[:half], second)
    row_panel = lax.all_gather(row_strip, "col", axis=1, tiled=True)
    leading = row_panel[:TILE]
    lead_second = lax.ppermute(leading[half:], "row", route)
    lead = lax.all_gather(jnp.where(upper, leading[:half], lead_second), "row")
    block = lead.reshape(2, STEPS, half, PIVOTS).transpose(1, 0, 2, 3).reshape(PIVOTS, PIVOTS)
    col_panel = lax.all_gather(shared, "row")
    col_panel = col_panel.reshape(2, STEPS, half, local_cols).transpose(1, 0, 2, 3).reshape(PIVOTS, local_cols)
    inverse = inverse_factor(block)
    solved = jnp.dot(row_panel, inverse.T, precision=HIGH)
    row_number = jnp.arange(local_rows, dtype=jnp.int32)[:, None]
    row_number = row_number // TILE * TILE * rows + row_index * TILE + row_number % TILE
    lower_panel = jnp.where(row_number >= jnp.arange(PIVOTS)[None, :], solved, 0.0)
    update_rows = jnp.where(row_number < PIVOTS, 0.0, solved)
    update_cols = jnp.dot(inverse, col_panel, precision=HIGH)
    update_cols = jnp.where(jnp.arange(local_cols)[None, :] < TILE, 0.0, update_cols)
    front_out = assembled - jnp.dot(update_rows, update_cols, precision=HIGH)
    return front_out, lower_panel


def solution(mesh):
    return jax.shard_map(
        per_device,
        mesh=mesh,
        in_specs=(P("row", "col"), P(None, "row", "col"), P()),
        out_specs=(P("row", "col"), P("row", None)),
        check_vma=False,
    )
```

```python
import jax
import jax.numpy as jnp
from jax import lax
from jax.experimental import pallas as pl
from jax.experimental.pallas import tpu as pltpu
from jax.sharding import PartitionSpec as P

f32 = jnp.float32
bf16 = jnp.bfloat16
TILE = 128
RUN = 16
PIVOTS = 1024
STEPS = PIVOTS // TILE
SUB = 8
GROUPS = TILE // SUB
ITEMS = 36
SHARE = 5
MIB = 2**20


def split2(x):
    hi = x.astype(bf16)
    return hi, (x - hi.astype(f32)).astype(bf16)


def split3(x):
    hi = x.astype(bf16).astype(f32)
    rest = x - hi
    mid = rest.astype(bf16).astype(f32)
    return hi, mid, rest - mid


def mm3(a, b, dims):
    ah, al = split2(a)
    bh, bl = split2(b)

    def dot(x, y):
        return lax.dot_general(x, y, (dims, ((), ())), preferred_element_type=f32)

    return dot(ah, bh) + (dot(ah, bl) + dot(al, bh))


def lane(x, k):
    return jnp.broadcast_to(x[:, k : k + 1], (SUB, TILE))


def sublane(x, k):
    return jnp.broadcast_to(x[k : k + 1, :], (SUB, TILE))


def factor_tile(a, e):
    row_of = lax.broadcasted_iota(jnp.int32, (SUB, TILE), 0)

    def packed(v):
        out = v[SUB - 1]
        for t in range(SUB - 2, -1, -1):
            out = jnp.where(row_of == t, v[t], out)
        return out

    inverse_rows = []
    last_u = last_e = None
    for b in range(GROUPS):
        r = [sublane(a[b], t) for t in range(SUB)]
        w = [sublane(e[b], t) for t in range(SUB)]
        if b:
            for s in range(SUB):
                for t in range(SUB):
                    factor = lane(last_u[t], SUB * b + s)
                    r[s] = r[s] - factor * last_u[t]
                    w[s] = w[s] - factor * last_e[t]
        d = [[lane(r[t], SUB * b + s) if s >= t else None for t in range(SUB)] for s in range(SUB)]
        u = [None] * SUB
        v = [None] * SUB
        for t in range(SUB):
            scale = lax.rsqrt(d[t][t])
            u[t] = r[t] * scale
            v[t] = w[t] * scale
            below = [d[s][t] * scale if s > t else None for s in range(SUB)]
            for s in range(t + 1, SUB):
                for q in range(t + 1, s + 1):
                    d[s][q] = d[s][q] - below[s] * below[q]
            for s in range(t + 1, SUB):
                r[s] = r[s] - below[s] * u[t]
                w[s] = w[s] - below[s] * v[t]
        last_u, last_e = u, v
        urows, erows = packed(u), packed(v)
        inverse_rows.append(erows)
        if b < GROUPS - 2:
            uh, um, ul = split3(urows)
            eh, em, el = split3(erows)
            left = jnp.concatenate([uh, uh, um, um, uh, ul], 0).astype(bf16)
            right = jnp.concatenate(
                [jnp.concatenate([uh, um, uh, um, ul, uh], 0), jnp.concatenate([eh, em, eh, em, el, eh], 0)], 1
            ).astype(bf16)
            change = lax.dot_general(left, right, (((0,), (0,)), ((), ())), preferred_element_type=f32)
            for i in range(b + 2, GROUPS):
                a[i] = a[i] - change[SUB * i : SUB * i + SUB, :TILE]
                e[i] = e[i] - change[SUB * i : SUB * i + SUB, TILE:]
    return jnp.concatenate(inverse_rows, 0)


def load_block(pivots, work):
    for x in range(2):
        for y in range(4):
            for z in range(4):
                for core in range(2):
                    i = x * 4 + y % 2 * 2 + core
                    j = y // 2 * 4 + z
                    work[i * TILE : (i + 1) * TILE, j * TILE : (j + 1) * TILE] = pivots[core, x, y, z]
    for i in range(STEPS):
        ri = lax.broadcasted_iota(jnp.int32, (TILE, PIVOTS), 0) + i * TILE
        ci = lax.broadcasted_iota(jnp.int32, (TILE, PIVOTS), 1)
        work[i * TILE : (i + 1) * TILE, PIVOTS:] = (ri == ci).astype(f32)


def factor_steps(work, between):
    width = (STEPS + 1) * TILE

    @pl.loop(0, STEPS)
    def _(k):
        between(k)
        kb = pl.ds(pl.multiple_of(k * TILE, TILE), TILE)
        window = pl.ds(pl.multiple_of(k * TILE, TILE), width)
        tile = work[kb, kb]
        ri = lax.broadcasted_iota(jnp.int32, (SUB, TILE), 0)
        ci = lax.broadcasted_iota(jnp.int32, (SUB, TILE), 1)
        a = [tile[SUB * i : SUB * i + SUB] for i in range(GROUPS)]
        e = [(ri + SUB * i == ci).astype(f32) for i in range(GROUPS)]
        inverse = factor_tile(a, e)
        work[kb, window] = mm3(inverse, work[kb, window], ((1,), (0,)))

        @pl.loop(k + 1, STEPS)
        def _(i):
            ib = pl.ds(pl.multiple_of(i * TILE, TILE), TILE)
            work[ib, window] -= mm3(work[kb, ib], work[kb, window], ((0,), (0,)))


class Exchange:
    def __init__(self, send_sems, recv_sems):
        self.send_sems, self.recv_sems, self.used = send_sems, recv_sems, 0
        self.sent = []

    def copy(self, ref, out_at, in_at, device, sends=None, receives=None, source=None):
        n = self.used
        self.used += 1

        def made(at, src):
            return pltpu.make_async_remote_copy(
                src_ref=src,
                dst_ref=ref.at[at],
                send_sem=self.send_sems.at[n],
                recv_sem=self.recv_sems.at[n],
                device_id=device,
                device_id_type=pl.DeviceIdType.MESH,
            )

        def start():
            made(out_at, ref.at[out_at] if source is None else source).start()

        def wait_recv():
            made(in_at, ref.at[in_at]).wait_recv()

        def wait_send():
            made(out_at, ref.at[out_at] if source is None else source).wait_send()

        self.sent.append((sends, wait_send))
        return (sends, start), (receives, wait_recv)

    def drain(self):
        for guard, wait in self.sent:
            guarded(guard, wait)


def guarded(guard, action):
    if guard is None:
        action()
    else:
        pl.when(guard)(action)


def begin(copies):
    for (guard, start), _ in copies:
        guarded(guard, start)
    return copies


def finish(copies):
    for _, (guard, wait) in copies:
        guarded(guard, wait)


def gather_kernel(strip_ref, cols_ref, xh_ref, xl_ref, wrow_ref, wcol_ref, pivots, work, send_sems, recv_sems):
    r, c = lax.axis_index("row"), lax.axis_index("col")
    x, yl, core = r // 4, r // 2 % 2, r % 2
    yh, z = c // 4, c % 4
    y = yh * 2 + yl
    at = {"x": x, "y": y, "z": z}
    near = x < 2
    xs = x % 2

    def device(x=x, y=y, z=z, core=core):
        return (x * 4 + y % 2 * 2 + core, y // 2 * 4 + z)

    def moved(dim, step):
        return (at[dim] + step) % 4

    barrier = pltpu.get_barrier_semaphore()
    for dim in "xyz":
        for step in range(1, 4):
            pl.semaphore_signal(
                barrier, inc=1, device_id=device(**{dim: moved(dim, step)}), device_id_type=pl.DeviceIdType.MESH
            )
    pl.semaphore_signal(barrier, inc=1, device_id=device(core=1 - core), device_id_type=pl.DeviceIdType.MESH)

    @pl.when(near)
    def _():
        pivots[core, xs, y, z] = strip_ref[:TILE, :]
        wcol_ref[r % 8] = cols_ref[...]

    wrow_ref[:, pl.ds(pl.multiple_of(c * TILE, TILE), TILE)] = strip_ref[...]
    pl.semaphore_wait(barrier, 10)
    ex = Exchange(send_sems, recv_sems)

    def pivot_phase(rows, order, number):
        dim, done = order[number], order[:number]
        waits = []
        for step in range(1, 4):

            def block(**over):
                place = {"x": xs, "y": y, "z": z, **over}
                full = {"x": pl.ds(0, 2), "y": pl.ds(0, 4), "z": pl.ds(0, 4)}
                index = [full[d] if d in done else place[d] for d in "xyz"]
                return (core, *index, pl.ds(rows[0], rows[1] - rows[0]))

            source = moved(dim, -step)
            if "x" in done:
                sends = receives = None
            elif dim == "x":
                sends, receives = near, source < 2
            else:
                sends = receives = near
            waits.append(
                ex.copy(
                    pivots,
                    block(),
                    block(**{dim: source % 2 if dim == "x" else source}),
                    device(**{dim: moved(dim, step)}),
                    sends,
                    receives,
                )
            )
        return begin(waits)

    def pivot_swap(rows):
        def block(k):
            full = (pl.ds(0, 2), pl.ds(0, 4), pl.ds(0, 4))
            return (k, *full, pl.ds(rows[0], rows[1] - rows[0]))

        return begin([ex.copy(pivots, block(core), block(1 - core), device(core=1 - core))])

    parts = (((0, 48), "xyz"), ((48, 96), "zxy"), ((96, 128), "yzx"))
    pending = [pivot_phase(rows, order, 0) for rows, order in parts]
    for number in (1, 2):
        for p, (rows, order) in enumerate(parts):
            finish(pending[p])
            pending[p] = pivot_phase(rows, order, number)
    for p, (rows, order) in enumerate(parts):
        finish(pending[p])
        pending[p] = pivot_swap(rows)

    low, high = (pl.ds(0, 512), pl.ds(512, 512))
    left, right = (pl.ds(0, 1024), pl.ds(1024, 1024))

    def tiles(first, count):
        return pl.ds(pl.multiple_of(first * TILE, TILE), count * TILE)

    def owner(x, yl):
        return x * 4 + yl * 2 + core

    first_row = [ex.copy(wrow_ref, (low, tiles(c, 1)), (low, tiles((c + 4) % 8, 1)), device(y=(y + 2) % 4))]
    second_row = [
        ex.copy(
            wrow_ref,
            (high, tiles(c, 1)),
            (high, tiles(yh * 4 + moved("z", -step), 1)),
            device(z=moved("z", step)),
        )
        for step in range(1, 4)
    ]
    first_col = [
        ex.copy(
            wcol_ref,
            (owner(xs, yl), pl.ds(0, TILE), left),
            (owner(moved("x", -step) % 2, yl), pl.ds(0, TILE), left),
            device(x=moved("x", step)),
            near,
            moved("x", -step) < 2,
        )
        for step in range(1, 4)
    ]
    y_pair = yh * 2 + 1 - yl
    second_col = [
        ex.copy(
            wcol_ref,
            (owner(xs, yl), pl.ds(0, TILE), right),
            (owner(xs, 1 - yl), pl.ds(0, TILE), right),
            device(y=y_pair),
            near,
            near,
        )
    ]
    for copies in (first_row, second_row, first_col, second_col):
        begin(copies)
    for p in range(3):
        finish(pending[p])
    load_block(pivots, work)
    last_row = [
        ex.copy(
            wrow_ref,
            (low, tiles(h * 4 + z, 1)),
            (low, tiles(h * 4 + moved("z", -step), 1)),
            device(z=moved("z", step)),
        )
        for step in range(1, 4)
        for h in range(2)
    ]
    side_row = [ex.copy(wrow_ref, (high, tiles(yh * 4, 4)), (high, tiles((1 - yh) * 4, 4)), device(y=(y + 2) % 4))]
    far_col = [
        ex.copy(
            wcol_ref,
            (owner(xs, h), pl.ds(0, TILE), right),
            (owner(moved("x", -step) % 2, h), pl.ds(0, TILE), right),
            device(x=moved("x", step)),
            near,
            moved("x", -step) < 2,
        )
        for step in range(1, 4)
        for h in range(2)
    ]
    side_col = [
        ex.copy(wcol_ref, (owner(h, yl), pl.ds(0, TILE), left), (owner(h, 1 - yl), pl.ds(0, TILE), left), device(y=y_pair))
        for h in range(2)
    ]
    swaps = [
        [
            ex.copy(
                wcol_ref,
                (4 * a + 2 * b + core, pl.ds(0, TILE), half),
                (4 * a + 2 * b + 1 - core, pl.ds(0, TILE), half),
                device(core=1 - core),
            )
            for a in range(2)
            for b in range(2)
        ]
        for half in (left, right)
    ]

    def middle():
        finish(first_row)
        begin(last_row)
        finish(second_row)
        begin(side_row)
        finish(second_col)
        begin(far_col)
        finish(first_col)
        begin(side_col)

    def swap_cols():
        for copies, swap in ((side_col, swaps[0]), (far_col, swaps[1])):
            finish(copies)
            begin(swap)

    def between(k):
        pl.when(k == 3)(middle)
        pl.when(k == 6)(swap_cols)

    if OVERLAP:
        factor_steps(work, between)
    else:
        middle()
        swap_cols()
        factor_steps(work, lambda k: None)
    finish(last_row)
    finish(side_row)
    finish(swaps[0])
    finish(swaps[1])
    ex.drain()
    for i in range(STEPS):
        rows = slice(i * TILE, (i + 1) * TILE)
        xh_ref[rows], xl_ref[rows] = split2(work[rows, PIVOTS:])


OVERLAP = True
COPIES = 80


def gather_and_factor(row_strip, col_strip):
    vmem = pl.BlockSpec(memory_space=pltpu.VMEM)
    local_rows, local_cols = row_strip.shape[0], col_strip.shape[1]
    half = jax.ShapeDtypeStruct((PIVOTS, PIVOTS), bf16)
    return pl.pallas_call(
        gather_kernel,
        out_shape=(
            half,
            half,
            jax.ShapeDtypeStruct((local_rows, PIVOTS), f32),
            jax.ShapeDtypeStruct((STEPS, TILE, local_cols), f32),
        ),
        in_specs=[vmem] * 2,
        out_specs=(vmem,) * 4,
        scratch_shapes=[
            pltpu.VMEM((2, 2, 4, 4, TILE, TILE), f32),
            pltpu.VMEM((PIVOTS, 2 * PIVOTS), f32),
            pltpu.SemaphoreType.DMA((COPIES,)),
            pltpu.SemaphoreType.DMA((COPIES,)),
        ],
        compiler_params=pltpu.CompilerParams(
            vmem_limit_bytes=48 * MIB, collective_id=0, has_side_effects=True
        ),
        cost_estimate=pl.CostEstimate(flops=5 * 10**10, bytes_accessed=8 * MIB, transcendentals=0),
        name="gather_factor",
    )(row_strip, col_strip)


def dot3(ah, al, bh, bl, dims):
    def dot(p, q):
        return lax.dot_general(p, q, (dims, ((), ())), preferred_element_type=f32)

    return dot(ah, bh) + (dot(ah, bl) + dot(al, bh))


QUARTER = 256


def solve_rows_kernel(place_ref, w_ref, xh_ref, xl_ref, lower_ref, uh_ref, ul_ref):
    step = pl.program_id(0)
    wh, wl = split2(w_ref[...])
    count = w_ref.shape[0]
    for n in range(PIVOTS // QUARTER):
        block = slice(n * QUARTER, (n + 1) * QUARTER)
        depth = slice(0, (n + 1) * QUARTER)
        b = dot3(wh[:, depth], wl[:, depth], xh_ref[block, depth], xl_ref[block, depth], ((1,), (1,)))
        row = lax.broadcasted_iota(jnp.int32, b.shape, 0)
        row = row % TILE + (row // TILE + step * (count // TILE)) * (TILE * place_ref[0]) + place_ref[1] * TILE
        col = lax.broadcasted_iota(jnp.int32, b.shape, 1) + n * QUARTER
        lower_ref[:, block] = jnp.where(row >= col, b, 0.0)
        uh_ref[:, block], ul_ref[:, block] = split2(jnp.where(row < PIVOTS, 0.0, b))


def solve_rows(place, panel, xh, xl):
    rows = panel.shape[0]
    whole = pl.BlockSpec((PIVOTS, PIVOTS), lambda i: (0, 0))
    block = pl.BlockSpec((QUARTER, PIVOTS), lambda i: (i, 0))
    half = jax.ShapeDtypeStruct((rows, PIVOTS), bf16)
    return pl.pallas_call(
        solve_rows_kernel,
        grid=(rows // QUARTER,),
        out_shape=(jax.ShapeDtypeStruct((rows, PIVOTS), f32), half, half),
        in_specs=[pl.BlockSpec(memory_space=pltpu.SMEM), block, whole, whole],
        out_specs=(block,) * 3,
        compiler_params=pltpu.CompilerParams(vmem_limit_bytes=40 * MIB),
        name="solve_rows",
    )(place, panel, xh, xl)


def update_kernel(front_ref, w_ref, xh_ref, xl_ref, uh_ref, ul_ref, out_ref, bh, bl):
    wh, wl = split2(w_ref[...].reshape(PIVOTS, QUARTER))
    for n in range(PIVOTS // QUARTER):
        block = slice(n * QUARTER, (n + 1) * QUARTER)
        depth = slice(0, (n + 1) * QUARTER)
        b = dot3(xh_ref[block, depth], xl_ref[block, depth], wh[depth], wl[depth], ((1,), (0,)))
        col = lax.broadcasted_iota(jnp.int32, b.shape, 1) + pl.program_id(0) * QUARTER
        bh[block], bl[block] = split2(jnp.where(col < TILE, 0.0, b))
    for n in range(front_ref.shape[0] // QUARTER):
        block = slice(n * QUARTER, (n + 1) * QUARTER)
        out_ref[block] = front_ref[block] - dot3(uh_ref[block], ul_ref[block], bh[...], bl[...], ((1,), (0,)))


def update(front, panel, xh, xl, uh, ul):
    rows, cols = front.shape
    whole = pl.BlockSpec((PIVOTS, PIVOTS), lambda j: (0, 0))
    rows_whole = pl.BlockSpec((rows, PIVOTS), lambda j: (0, 0))
    block = pl.BlockSpec((rows, QUARTER), lambda j: (0, j))
    return pl.pallas_call(
        update_kernel,
        grid=(cols // QUARTER,),
        out_shape=jax.ShapeDtypeStruct(front.shape, f32),
        in_specs=[block, pl.BlockSpec((STEPS, TILE, QUARTER), lambda j: (0, 0, j)), whole, whole, rows_whole, rows_whole],
        out_specs=block,
        scratch_shapes=[pltpu.VMEM((PIVOTS, QUARTER), bf16)] * 2,
        compiler_params=pltpu.CompilerParams(vmem_limit_bytes=40 * MIB),
        name="update",
    )(front, panel, xh, xl, uh, ul)


def reorder_kernel(index_ref, in_ref, out_ref):
    @pl.loop(0, in_ref.shape[0])
    def _(d):
        for m in range(SHARE):
            out_ref[d, m] = in_ref[index_ref[d, m], m]


def reorder(pieces, index):
    vmem = pl.BlockSpec(memory_space=pltpu.VMEM)
    return pl.pallas_call(
        reorder_kernel,
        out_shape=jax.ShapeDtypeStruct(pieces.shape, f32),
        in_specs=[pl.BlockSpec(memory_space=pltpu.SMEM), vmem],
        out_specs=vmem,
        compiler_params=pltpu.CompilerParams(vmem_limit_bytes=16 * MIB),
        name="reorder",
    )(index, pieces)


def relay(children, child_map, rows, cols, row_index, col_index):
    pieces = children.reshape(2, 3, rows, SUB, 6, TILE).transpose(2, 0, 1, 4, 3, 5).reshape(rows, ITEMS, SUB, TILE)
    pieces = jnp.pad(pieces, ((0, 0), (0, cols * SHARE - ITEMS), (0, 0), (0, 0)))
    pieces = pieces.reshape(rows * cols, SHARE, SUB, TILE)
    held = lax.all_to_all(pieces, ("row", "col"), 0, 0, tiled=True)
    item = jnp.minimum(col_index * SHARE + jnp.arange(SHARE), ITEMS - 1)
    child, run, tile = item // 18, item % 18 // 6, item % 6
    row_start = child_map[child, run * RUN]
    col_start = child_map[child, tile // 2 * RUN]
    target = jnp.arange(rows * cols, dtype=jnp.int32)[:, None]
    index = (target // cols - row_start) % rows * cols + (target % cols - col_start) % cols
    held = reorder(held, index.astype(jnp.int32))
    back = lax.all_to_all(held, ("row", "col"), 0, 0, tiled=True)
    return back.reshape(rows, cols * SHARE, SUB, TILE)[:, :ITEMS]


def assemble_kernel(slots_ref, front_ref, items_ref, out_ref):
    out_ref[...] = front_ref[...]
    for m in range(ITEMS):
        row = pl.ds(pl.multiple_of(slots_ref[0, m] * TILE, TILE), TILE)
        col = pl.ds(pl.multiple_of(slots_ref[1, m] * TILE, TILE), TILE)
        out_ref[row, col] += items_ref[:, m].reshape(TILE, TILE)


def assemble(front, items, child_map, rows, cols, row_index, col_index):
    item = jnp.arange(ITEMS)
    child, run, tile = item // 18, item % 18 // 6, item % 6
    row_start = child_map[child, run * RUN]
    col_start = child_map[child, tile // 2 * RUN]
    row_slot = (row_start + (row_index - row_start) % rows) // rows
    col_slot = (col_start + (col_index - col_start) % cols) // cols + tile % 2
    slots = jnp.stack([row_slot, col_slot]).astype(jnp.int32)
    vmem = pl.BlockSpec(memory_space=pltpu.VMEM)
    return pl.pallas_call(
        assemble_kernel,
        out_shape=jax.ShapeDtypeStruct(front.shape, f32),
        in_specs=[pl.BlockSpec(memory_space=pltpu.SMEM), vmem, vmem],
        out_specs=vmem,
        compiler_params=pltpu.CompilerParams(vmem_limit_bytes=32 * MIB),
        name="assemble",
    )(slots, front, items)


def per_device(front, children, child_map):
    rows, cols = lax.axis_size("row"), lax.axis_size("col")
    row_index, col_index = lax.axis_index("row"), lax.axis_index("col")
    local_rows, local_cols = front.shape
    items = relay(children, child_map, rows, cols, row_index, col_index)
    assembled = assemble(front, items, child_map, rows, cols, row_index, col_index)
    xh, xl, row_panel, col_panel = gather_and_factor(assembled[:, :TILE], assembled[:TILE, :])
    place = jnp.stack([jnp.int32(rows), row_index])
    lower_panel, uh, ul = solve_rows(place, row_panel, xh, xl)
    front_out = update(assembled, col_panel, xh, xl, uh, ul)
    return front_out, lower_panel


def solution(mesh):
    return jax.shard_map(
        per_device,
        mesh=mesh,
        in_specs=(P("row", "col"), P(None, "row", "col"), P()),
        out_specs=(P("row", "col"), P("row", None)),
        check_vma=False,
    )
```

```python
import jax
import jax.numpy as jnp
from jax import lax
from jax.experimental import pallas as pl
from jax.experimental.pallas import tpu as pltpu
from jax.sharding import PartitionSpec as P

f32 = jnp.float32
bf16 = jnp.bfloat16
TILE = 128
RUN = 16
PIVOTS = 1024
STEPS = PIVOTS // TILE
SUB = 8
STRIDE1 = 29
STRIDE2 = 37
GROUPS = TILE // SUB
MIB = 2**20


def split2(x):
    hi = x.astype(bf16)
    return hi, (x - hi.astype(f32)).astype(bf16)


def split3(x):
    hi = x.astype(bf16).astype(f32)
    rest = x - hi
    mid = rest.astype(bf16).astype(f32)
    return hi, mid, rest - mid


def mm3(a, b, dims):
    ah, al = split2(a)
    bh, bl = split2(b)

    def dot(x, y):
        return lax.dot_general(x, y, (dims, ((), ())), preferred_element_type=f32)

    return dot(ah, bh) + (dot(ah, bl) + dot(al, bh))


def lane(x, k):
    return jnp.broadcast_to(x[:, k : k + 1], (SUB, TILE))


def sublane(x, k):
    return jnp.broadcast_to(x[k : k + 1, :], (SUB, TILE))


def factor_tile(a, e):
    row_of = lax.broadcasted_iota(jnp.int32, (SUB, TILE), 0)

    def packed(v):
        out = v[SUB - 1]
        for t in range(SUB - 2, -1, -1):
            out = jnp.where(row_of == t, v[t], out)
        return out

    inverse_rows = []
    last_u = last_e = None
    for b in range(GROUPS):
        r = [sublane(a[b], t) for t in range(SUB)]
        w = [sublane(e[b], t) for t in range(SUB)]
        if b:
            for s in range(SUB):
                for t in range(SUB):
                    factor = lane(last_u[t], SUB * b + s)
                    r[s] = r[s] - factor * last_u[t]
                    w[s] = w[s] - factor * last_e[t]
        d = [[lane(r[t], SUB * b + s) if s >= t else None for t in range(SUB)] for s in range(SUB)]
        u = [None] * SUB
        v = [None] * SUB
        for t in range(SUB):
            scale = lax.rsqrt(d[t][t])
            u[t] = r[t] * scale
            v[t] = w[t] * scale
            below = [d[s][t] * scale if s > t else None for s in range(SUB)]
            for s in range(t + 1, SUB):
                for q in range(t + 1, s + 1):
                    d[s][q] = d[s][q] - below[s] * below[q]
            for s in range(t + 1, SUB):
                r[s] = r[s] - below[s] * u[t]
                w[s] = w[s] - below[s] * v[t]
        last_u, last_e = u, v
        urows, erows = packed(u), packed(v)
        inverse_rows.append(erows)
        if b < GROUPS - 2:
            uh, um, ul = split3(urows)
            eh, em, el = split3(erows)
            left = jnp.concatenate([uh, uh, um, um, uh, ul], 0).astype(bf16)
            right = jnp.concatenate(
                [jnp.concatenate([uh, um, uh, um, ul, uh], 0), jnp.concatenate([eh, em, eh, em, el, eh], 0)], 1
            ).astype(bf16)
            change = lax.dot_general(left, right, (((0,), (0,)), ((), ())), preferred_element_type=f32)
            for i in range(b + 2, GROUPS):
                a[i] = a[i] - change[SUB * i : SUB * i + SUB, :TILE]
                e[i] = e[i] - change[SUB * i : SUB * i + SUB, TILE:]
    return jnp.concatenate(inverse_rows, 0)


def load_block(pivots, work):
    for x in range(2):
        for y in range(4):
            for z in range(4):
                for core in range(2):
                    i = x * 4 + y % 2 * 2 + core
                    j = y // 2 * 4 + z
                    work[i * TILE : (i + 1) * TILE, j * TILE : (j + 1) * TILE] = pivots[core, x, y, z]
    for i in range(STEPS):
        ri = lax.broadcasted_iota(jnp.int32, (TILE, PIVOTS), 0) + i * TILE
        ci = lax.broadcasted_iota(jnp.int32, (TILE, PIVOTS), 1)
        work[i * TILE : (i + 1) * TILE, PIVOTS:] = (ri == ci).astype(f32)


def factor_steps(work, between):
    width = (STEPS + 1) * TILE

    @pl.loop(0, STEPS)
    def _(k):
        between(k)
        kb = pl.ds(pl.multiple_of(k * TILE, TILE), TILE)
        window = pl.ds(pl.multiple_of(k * TILE, TILE), width)
        tile = work[kb, kb]
        ri = lax.broadcasted_iota(jnp.int32, (SUB, TILE), 0)
        ci = lax.broadcasted_iota(jnp.int32, (SUB, TILE), 1)
        a = [tile[SUB * i : SUB * i + SUB] for i in range(GROUPS)]
        e = [(ri + SUB * i == ci).astype(f32) for i in range(GROUPS)]
        inverse = factor_tile(a, e)
        work[kb, window] = mm3(inverse, work[kb, window], ((1,), (0,)))

        @pl.loop(k + 1, STEPS)
        def _(i):
            ib = pl.ds(pl.multiple_of(i * TILE, TILE), TILE)
            work[ib, window] -= mm3(work[kb, ib], work[kb, window], ((0,), (0,)))


class Exchange:
    def __init__(self, send_sems, recv_sems):
        self.send_sems, self.recv_sems, self.used = send_sems, recv_sems, 0
        self.sent = []

    def copy(self, ref, out_at, in_at, device, sends=None, receives=None, source=None):
        n = self.used
        self.used += 1

        def made(at, src):
            return pltpu.make_async_remote_copy(
                src_ref=src,
                dst_ref=ref.at[at],
                send_sem=self.send_sems.at[n],
                recv_sem=self.recv_sems.at[n],
                device_id=device,
                device_id_type=pl.DeviceIdType.MESH,
            )

        def start():
            made(out_at, ref.at[out_at] if source is None else source).start()

        def wait_recv():
            made(in_at, ref.at[in_at]).wait_recv()

        def wait_send():
            made(out_at, ref.at[out_at] if source is None else source).wait_send()

        self.sent.append((sends, wait_send))
        return (sends, start), (receives, wait_recv)

    def drain(self):
        for guard, wait in self.sent:
            guarded(guard, wait)


def guarded(guard, action):
    if guard is None:
        action()
    else:
        pl.when(guard)(action)


def begin(copies):
    for (guard, start), _ in copies:
        guarded(guard, start)
    return copies


def finish(copies):
    for _, (guard, wait) in copies:
        guarded(guard, wait)


def relay(r, c, rows, cols, map_ref, child_ref, moved_ref, held, turned, sems):
    groups = 2 * 3
    me = r * cols + c
    group = (c + cols - 2 * r % cols) % cols
    holds = group < groups
    child, run = group // 3 % 2, group % 3
    count = rows * groups

    def column(k, g):
        return (g + 2 * k) % cols

    def rows_of(g, k):
        return pl.ds(pl.multiple_of(g % 3 * TILE + k * SUB, SUB), SUB)

    def first(k, g):
        return pltpu.make_async_remote_copy(
            src_ref=child_ref.at[g // 3, rows_of(g, k)],
            dst_ref=held.at[me],
            send_sem=sems.at[0],
            recv_sem=sems.at[1],
            device_id=(k, column(k, g)),
            device_id_type=pl.DeviceIdType.MESH,
        )

    def second(e):
        return pltpu.make_async_remote_copy(
            src_ref=turned.at[e],
            dst_ref=moved_ref.at[child, rows_of(group, r)],
            send_sem=sems.at[2],
            recv_sem=sems.at[3],
            device_id=(e // cols, e % cols),
            device_id_type=pl.DeviceIdType.MESH,
        )

    def all_of(ref, n):
        return ref.at[pl.ds(0, n)]

    def waiting(n, sem):
        return pltpu.make_async_copy(all_of(held, n), all_of(turned, n), sem)

    @pl.loop(0, count)
    def _(i):
        j = i * STRIDE1 % count
        k, g = (r + j // groups) % rows, (j + c) % groups

        @pl.when(k * cols + column(k, g) != me)
        def _():
            first(k, g).start()

    @pl.when(holds)
    def _():
        held[me] = child_ref[child, rows_of(group, r)]
        waiting(rows * cols - 1, sems.at[1]).wait()
        row_start = map_ref[child, run * RUN]
        col_starts = [map_ref[child, n * RUN] for n in range(3)]

        @pl.loop(0, rows * cols)
        def _(i):
            e = (me + i * STRIDE2) % (rows * cols)
            source = (e // cols + 2 * TILE - row_start) % rows * cols
            for n in range(3):
                part = slice(n * 2 * TILE, (n + 1) * 2 * TILE)
                turned[e, :, part] = held[source + (e % cols + 2 * TILE - col_starts[n]) % cols, :, part]

            @pl.when(i > 0)
            def _():
                second(e).start()

        moved_ref[child, rows_of(group, r)] = turned[me]
        waiting(count - 1, sems.at[0]).wait()
        waiting(rows * cols - 1, sems.at[2]).wait()
        waiting(count - 1, sems.at[3]).wait()

    @pl.when(group >= groups)
    def _():
        waiting(count, sems.at[0]).wait()
        waiting(count, sems.at[3]).wait()


def gather_kernel(
    map_ref, strip_ref, cols_ref, child_ref, xh_ref, xl_ref, wrow_ref, wcol_ref, moved_ref,
    held, turned, pivots, work, relay_sems, send_sems, recv_sems,
):
    rows, cols = lax.axis_size("row"), lax.axis_size("col")
    r, c = lax.axis_index("row"), lax.axis_index("col")
    x, yl, core = r // 4, r // 2 % 2, r % 2
    yh, z = c // 4, c % 4
    y = yh * 2 + yl
    at = {"x": x, "y": y, "z": z}
    near = x < 2
    xs = x % 2

    def device(x=x, y=y, z=z, core=core):
        return (x * 4 + y % 2 * 2 + core, y // 2 * 4 + z)

    def moved(dim, step):
        return (at[dim] + step) % 4

    barrier = pltpu.get_barrier_semaphore()

    @pl.loop(1, rows * cols)
    def _(i):
        e = (r * cols + c + i) % (rows * cols)
        pl.semaphore_signal(barrier, inc=1, device_id=(e // cols, e % cols), device_id_type=pl.DeviceIdType.MESH)

    pl.semaphore_wait(barrier, rows * cols - 1)
    relay(r, c, rows, cols, map_ref, child_ref, moved_ref, held, turned, relay_sems)

    def kept(condition, value):
        return jnp.where(condition, value, jnp.zeros_like(value))

    own_cols = pl.ds(pl.multiple_of(c * TILE, TILE), TILE)
    for slot in range(rows // 2):
        block = slice(slot * TILE, (slot + 1) * TILE)
        total = strip_ref[block, :]
        for child in range(2):
            inside = c >= map_ref[child, 0]
            for run in range(3):
                offset = slot * rows + r - map_ref[child, run * RUN]
                total = total + kept(
                    inside & (offset >= 0) & (offset < RUN), moved_ref[child, run * TILE : (run + 1) * TILE, :TILE]
                )
        wrow_ref[block, own_cols] = total

    @pl.when(near)
    def _():
        pivots[core, xs, y, z] = wrow_ref[:TILE, own_cols]
        for slot in range(2 * cols):
            block = slice(slot * TILE, (slot + 1) * TILE)
            total = cols_ref[:, block]
            for child in range(2):
                inside = r >= map_ref[child, 0]
                for tile in range(6):
                    offset = slot * cols + c - map_ref[child, tile // 2 * RUN] - tile % 2 * cols
                    total = total + kept(
                        inside & (offset >= 0) & (offset < cols),
                        moved_ref[child, :TILE, tile * TILE : (tile + 1) * TILE],
                    )
            wcol_ref[r % 8, :, block] = total

    ex = Exchange(send_sems, recv_sems)

    def pivot_phase(rows, order, number):
        dim, done = order[number], order[:number]
        waits = []
        for step in range(1, 4):

            def block(**over):
                place = {"x": xs, "y": y, "z": z, **over}
                full = {"x": pl.ds(0, 2), "y": pl.ds(0, 4), "z": pl.ds(0, 4)}
                index = [full[d] if d in done else place[d] for d in "xyz"]
                return (core, *index, pl.ds(rows[0], rows[1] - rows[0]))

            source = moved(dim, -step)
            if "x" in done:
                sends = receives = None
            elif dim == "x":
                sends, receives = near, source < 2
            else:
                sends = receives = near
            waits.append(
                ex.copy(
                    pivots,
                    block(),
                    block(**{dim: source % 2 if dim == "x" else source}),
                    device(**{dim: moved(dim, step)}),
                    sends,
                    receives,
                )
            )
        return begin(waits)

    def pivot_swap(rows):
        def block(k):
            full = (pl.ds(0, 2), pl.ds(0, 4), pl.ds(0, 4))
            return (k, *full, pl.ds(rows[0], rows[1] - rows[0]))

        return begin([ex.copy(pivots, block(core), block(1 - core), device(core=1 - core))])

    def tiles(first, count):
        return pl.ds(pl.multiple_of(first * TILE, TILE), count * TILE)

    def panel_row(rows, first, count, first_in, device):
        return ex.copy(wrow_ref, (rows, tiles(first, count)), (rows, tiles(first_in, count)), device)

    def panel_col(chunk, out, into, device, sends=None, receives=None):
        return ex.copy(
            wcol_ref, (out, pl.ds(0, TILE), chunk), (into, pl.ds(0, TILE), chunk), device, sends, receives
        )

    def owner(x, yl, core=core):
        return x * 4 + yl * 2 + core

    y_far = device(y=(y + 2) % 4)
    y_pair = device(y=yh * 2 + 1 - yl)
    x_pair = device(x=(5 - x) % 4)
    sibling = device(core=1 - core)
    top, bottom = pl.ds(0, ROW_SPLIT), pl.ds(ROW_SPLIT, strip_ref.shape[0] - ROW_SPLIT)
    top_first = [panel_row(top, c, 1, (c + cols // 2) % cols, y_far)]
    bottom_first = [
        panel_row(bottom, c, 1, yh * 4 + moved("z", -step), device(z=moved("z", step))) for step in range(1, 4)
    ]
    top_last = [
        panel_row(top, h * 4 + z, 1, h * 4 + moved("z", -step), device(z=moved("z", step)))
        for step in (1, 3, 2)
        for h in range(2)
    ]
    bottom_last = [panel_row(bottom, yh * 4, 4, (1 - yh) * 4, y_far)]

    def beside(chunk, halves):
        return [
            panel_col(
                chunk,
                owner(xs, h),
                owner(moved("x", -step) % 2, h),
                device(x=moved("x", step)),
                near,
                moved("x", -step) < 2,
            )
            for step in (1, 3)
            for h in halves
        ]

    def onward(chunk, halves):
        far = x >= 2
        return [panel_col(chunk, owner((x + 1) % 2, h), owner(xs, h), x_pair, far, far) for h in halves]

    def swapped(chunk):
        return [
            panel_col(chunk, owner(a, b), owner(a, b, 1 - core), sibling) for a in range(2) for b in range(2)
        ]

    chunks = [pl.ds(TILE + n * 5 * TILE, 5 * TILE) for n in range(3)]
    both = (0, 1)
    a_x, a_on = beside(chunks[0], (yl,)), onward(chunks[0], (yl,))
    a_y = [panel_col(chunks[0], owner(h, yl), owner(h, 1 - yl), y_pair) for h in both]
    b_y, c_y = ([panel_col(chunks[n], owner(xs, yl), owner(xs, 1 - yl), y_pair, near, near)] for n in (1, 2))
    b_x, c_x = (beside(chunks[n], both) for n in (1, 2))
    b_on, c_on = (onward(chunks[n], both) for n in (1, 2))
    swaps = [swapped(chunk) for chunk in chunks]

    parts = (((0, 48), "xyz"), ((48, 96), "zxy"), ((96, 128), "yzx"))
    pending = [pivot_phase(rows, order, 0) for rows, order in parts]
    for number in (1, 2):
        for p, (rows, order) in enumerate(parts):
            finish(pending[p])
            pending[p] = pivot_phase(rows, order, number)
        if number == EARLY:
            for copies in (a_x, b_y, bottom_first, c_y, top_first):
                begin(copies)
    for p, (rows, order) in enumerate(parts):
        finish(pending[p])
        pending[p] = pivot_swap(rows)
    for p in range(3):
        finish(pending[p])
    load_block(pivots, work)

    def then(before, after):
        finish(before)
        begin(after)

    plan = {
        1: [(a_x, a_on)],
        2: [(b_y, b_x), (top_first, top_last)],
        3: [(a_on, a_y), (bottom_first, bottom_last)],
        4: [(c_y, c_x)],
        5: [(b_x, b_on)],
        6: [(a_y, swaps[0])],
        7: [(c_x, c_on)],
    }

    def between(k):
        for step, pairs in plan.items():

            @pl.when(k == step)
            def _():
                for before, after in pairs:
                    then(before, after)

    factor_steps(work, between)
    then(b_on, swaps[1])
    then(c_on, swaps[2])
    for copies in (top_last, bottom_last, *swaps):
        finish(copies)
    ex.drain()
    for i in range(STEPS):
        rows = slice(i * TILE, (i + 1) * TILE)
        xh_ref[rows], xl_ref[rows] = split2(work[rows, PIVOTS:])


ROW_SPLIT = 768
EARLY = 2
COPIES = 80


def gather_and_factor(child_map, row_strip, col_strip, children):
    vmem = pl.BlockSpec(memory_space=pltpu.VMEM)
    local_rows, local_cols = row_strip.shape[0], col_strip.shape[1]
    half = jax.ShapeDtypeStruct((PIVOTS, PIVOTS), bf16)
    slices = (lax.axis_size("row") * lax.axis_size("col"), SUB, children.shape[2])
    return pl.pallas_call(
        gather_kernel,
        out_shape=(
            half,
            half,
            jax.ShapeDtypeStruct((local_rows, PIVOTS), f32),
            jax.ShapeDtypeStruct((STEPS, TILE, local_cols), f32),
            jax.ShapeDtypeStruct(children.shape, f32),
        ),
        in_specs=[pl.BlockSpec(memory_space=pltpu.SMEM)] + [vmem] * 3,
        out_specs=(vmem,) * 5,
        scratch_shapes=[
            pltpu.VMEM(slices, f32),
            pltpu.VMEM(slices, f32),
            pltpu.VMEM((2, 2, 4, 4, TILE, TILE), f32),
            pltpu.VMEM((PIVOTS, 2 * PIVOTS), f32),
            pltpu.SemaphoreType.DMA((4,)),
            pltpu.SemaphoreType.DMA((COPIES,)),
            pltpu.SemaphoreType.DMA((COPIES,)),
        ],
        compiler_params=pltpu.CompilerParams(
            vmem_limit_bytes=56 * MIB, collective_id=0, has_side_effects=True
        ),
        cost_estimate=pl.CostEstimate(flops=5 * 10**10, bytes_accessed=8 * MIB, transcendentals=0),
        name="gather_factor",
    )(child_map, row_strip, col_strip, children)


def dot3(ah, al, bh, bl, dims):
    def dot(p, q):
        return lax.dot_general(p, q, (dims, ((), ())), preferred_element_type=f32)

    return dot(ah, bh) + (dot(ah, bl) + dot(al, bh))


QUARTER = 256


def solve_rows_kernel(place_ref, w_ref, xh_ref, xl_ref, lower_ref, uh_ref, ul_ref):
    step = pl.program_id(0)
    wh, wl = split2(w_ref[...])
    count = w_ref.shape[0]
    for n in range(PIVOTS // QUARTER):
        block = slice(n * QUARTER, (n + 1) * QUARTER)
        depth = slice(0, (n + 1) * QUARTER)
        b = dot3(wh[:, depth], wl[:, depth], xh_ref[block, depth], xl_ref[block, depth], ((1,), (1,)))
        row = lax.broadcasted_iota(jnp.int32, b.shape, 0)
        row = row % TILE + (row // TILE + step * (count // TILE)) * (TILE * place_ref[0]) + place_ref[1] * TILE
        col = lax.broadcasted_iota(jnp.int32, b.shape, 1) + n * QUARTER
        lower_ref[:, block] = jnp.where(row >= col, b, 0.0)
        uh_ref[:, block], ul_ref[:, block] = split2(jnp.where(row < PIVOTS, 0.0, b))


def solve_rows(place, panel, xh, xl):
    rows = panel.shape[0]
    whole = pl.BlockSpec((PIVOTS, PIVOTS), lambda i: (0, 0))
    block = pl.BlockSpec((QUARTER, PIVOTS), lambda i: (i, 0))
    half = jax.ShapeDtypeStruct((rows, PIVOTS), bf16)
    return pl.pallas_call(
        solve_rows_kernel,
        grid=(rows // QUARTER,),
        out_shape=(jax.ShapeDtypeStruct((rows, PIVOTS), f32), half, half),
        in_specs=[pl.BlockSpec(memory_space=pltpu.SMEM), block, whole, whole],
        out_specs=(block,) * 3,
        compiler_params=pltpu.CompilerParams(vmem_limit_bytes=40 * MIB),
        name="solve_rows",
    )(place, panel, xh, xl)


def update_kernel(slots_ref, front_ref, moved_ref, w_ref, xh_ref, xl_ref, uh_ref, ul_ref, out_ref, bh, bl):
    wh, wl = split2(w_ref[...].reshape(PIVOTS, QUARTER))
    for n in range(PIVOTS // QUARTER):
        block = slice(n * QUARTER, (n + 1) * QUARTER)
        depth = slice(0, (n + 1) * QUARTER)
        b = dot3(xh_ref[block, depth], xl_ref[block, depth], wh[depth], wl[depth], ((1,), (0,)))
        col = lax.broadcasted_iota(jnp.int32, b.shape, 1) + pl.program_id(0) * QUARTER
        bh[block], bl[block] = split2(jnp.where(col < TILE, 0.0, b))
    for n in range(front_ref.shape[0] // QUARTER):
        block = slice(n * QUARTER, (n + 1) * QUARTER)
        out_ref[block] = front_ref[block] - dot3(uh_ref[block], ul_ref[block], bh[...], bl[...], ((1,), (0,)))
    for child in range(2):
        for tile in range(6):
            slot = slots_ref[1, child * 6 + tile]

            @pl.when(slot // (QUARTER // TILE) == pl.program_id(0))
            def _():
                col = pl.ds(pl.multiple_of(slot % (QUARTER // TILE) * TILE, TILE), TILE)
                for run in range(3):
                    row = pl.ds(pl.multiple_of(slots_ref[0, child * 3 + run] * TILE, TILE), TILE)
                    out_ref[row, col] += moved_ref[child, run * TILE : (run + 1) * TILE, tile * TILE : (tile + 1) * TILE]


def update(slots, front, moved, panel, xh, xl, uh, ul):
    rows, cols = front.shape
    whole = pl.BlockSpec((PIVOTS, PIVOTS), lambda j: (0, 0))
    rows_whole = pl.BlockSpec((rows, PIVOTS), lambda j: (0, 0))
    block = pl.BlockSpec((rows, QUARTER), lambda j: (0, j))
    return pl.pallas_call(
        update_kernel,
        grid=(cols // QUARTER,),
        out_shape=jax.ShapeDtypeStruct(front.shape, f32),
        in_specs=[
            pl.BlockSpec(memory_space=pltpu.SMEM),
            block,
            pl.BlockSpec(moved.shape, lambda j: (0, 0, 0)),
            pl.BlockSpec((STEPS, TILE, QUARTER), lambda j: (0, 0, j)),
            whole,
            whole,
            rows_whole,
            rows_whole,
        ],
        out_specs=block,
        scratch_shapes=[pltpu.VMEM((PIVOTS, QUARTER), bf16)] * 2,
        compiler_params=pltpu.CompilerParams(vmem_limit_bytes=40 * MIB),
        name="update",
    )(slots, front, moved, panel, xh, xl, uh, ul)


def per_device(front, children, child_map):
    rows, cols = lax.axis_size("row"), lax.axis_size("col")
    row_index, col_index = lax.axis_index("row"), lax.axis_index("col")
    xh, xl, row_panel, col_panel, moved = gather_and_factor(child_map, front[:, :TILE], front[:TILE, :], children)
    place = jnp.stack([jnp.int32(rows), row_index])
    lower_panel, uh, ul = solve_rows(place, row_panel, xh, xl)
    starts = child_map[:, ::RUN]
    row_slots = (starts + (row_index - starts) % rows) // rows
    col_slots = (starts + (col_index - starts) % cols) // cols
    col_slots = col_slots[:, :, None] + jnp.arange(RUN // cols)[None, None, :]
    slots = jnp.zeros((2, 12), jnp.int32).at[0, :6].set(row_slots.reshape(-1)).at[1].set(col_slots.reshape(-1))
    front_out = update(slots, front, moved, col_panel, xh, xl, uh, ul)
    return front_out, lower_panel


def solution(mesh):
    return jax.shard_map(
        per_device,
        mesh=mesh,
        in_specs=(P("row", "col"), P(None, "row", "col"), P()),
        out_specs=(P("row", "col"), P("row", None)),
        check_vma=False,
    )
```

```python
import jax
import jax.numpy as jnp
from jax import lax
from jax.experimental import pallas as pl
from jax.experimental.pallas import tpu as pltpu
from jax.sharding import PartitionSpec as P

f32 = jnp.float32
bf16 = jnp.bfloat16
TILE = 128
RUN = 16
PIVOTS = 1024
STEPS = PIVOTS // TILE
SUB = 8
STRIDE1 = 29
STRIDE2 = 37
GROUPS = TILE // SUB
MIB = 2**20


def split2(x):
    hi = x.astype(bf16)
    return hi, (x - hi.astype(f32)).astype(bf16)


def split3(x):
    hi = x.astype(bf16).astype(f32)
    rest = x - hi
    mid = rest.astype(bf16).astype(f32)
    return hi, mid, rest - mid


def mm3(a, b, dims):
    ah, al = split2(a)
    bh, bl = split2(b)

    def dot(x, y):
        return lax.dot_general(x, y, (dims, ((), ())), preferred_element_type=f32)

    return dot(ah, bh) + (dot(ah, bl) + dot(al, bh))


def lane(x, k):
    return jnp.broadcast_to(x[:, k : k + 1], (SUB, TILE))


def sublane(x, k):
    return jnp.broadcast_to(x[k : k + 1, :], (SUB, TILE))


def factor_tile(a, e):
    row_of = lax.broadcasted_iota(jnp.int32, (SUB, TILE), 0)

    def packed(v):
        out = v[SUB - 1]
        for t in range(SUB - 2, -1, -1):
            out = jnp.where(row_of == t, v[t], out)
        return out

    inverse_rows = []
    last_u = last_e = None
    for b in range(GROUPS):
        r = [sublane(a[b], t) for t in range(SUB)]
        w = [sublane(e[b], t) for t in range(SUB)]
        if b:
            for s in range(SUB):
                for t in range(SUB):
                    factor = lane(last_u[t], SUB * b + s)
                    r[s] = r[s] - factor * last_u[t]
                    w[s] = w[s] - factor * last_e[t]
        d = [[lane(r[t], SUB * b + s) if s >= t else None for t in range(SUB)] for s in range(SUB)]
        u = [None] * SUB
        v = [None] * SUB
        for t in range(SUB):
            scale = lax.rsqrt(d[t][t])
            u[t] = r[t] * scale
            v[t] = w[t] * scale
            below = [d[s][t] * scale if s > t else None for s in range(SUB)]
            for s in range(t + 1, SUB):
                for q in range(t + 1, s + 1):
                    d[s][q] = d[s][q] - below[s] * below[q]
            for s in range(t + 1, SUB):
                r[s] = r[s] - below[s] * u[t]
                w[s] = w[s] - below[s] * v[t]
        last_u, last_e = u, v
        urows, erows = packed(u), packed(v)
        inverse_rows.append(erows)
        if b < GROUPS - 2:
            uh, um, ul = split3(urows)
            eh, em, el = split3(erows)
            left = jnp.concatenate([uh, uh, um, um, uh, ul], 0).astype(bf16)
            right = jnp.concatenate(
                [jnp.concatenate([uh, um, uh, um, ul, uh], 0), jnp.concatenate([eh, em, eh, em, el, eh], 0)], 1
            ).astype(bf16)
            change = lax.dot_general(left, right, (((0,), (0,)), ((), ())), preferred_element_type=f32)
            for i in range(b + 2, GROUPS):
                a[i] = a[i] - change[SUB * i : SUB * i + SUB, :TILE]
                e[i] = e[i] - change[SUB * i : SUB * i + SUB, TILE:]
    return jnp.concatenate(inverse_rows, 0)


def load_block(pivots, work):
    for x in range(2):
        for y in range(4):
            for z in range(4):
                for core in range(2):
                    i = x * 4 + y % 2 * 2 + core
                    j = y // 2 * 4 + z
                    work[i * TILE : (i + 1) * TILE, j * TILE : (j + 1) * TILE] = pivots[core, x, y, z]
    for i in range(STEPS):
        ri = lax.broadcasted_iota(jnp.int32, (TILE, PIVOTS), 0) + i * TILE
        ci = lax.broadcasted_iota(jnp.int32, (TILE, PIVOTS), 1)
        work[i * TILE : (i + 1) * TILE, PIVOTS:] = (ri == ci).astype(f32)


def factor_steps(work, between):
    width = (STEPS + 1) * TILE

    @pl.loop(0, STEPS)
    def _(k):
        between(k, 0)
        kb = pl.ds(pl.multiple_of(k * TILE, TILE), TILE)
        window = pl.ds(pl.multiple_of(k * TILE, TILE), width)
        tile = work[kb, kb]
        ri = lax.broadcasted_iota(jnp.int32, (SUB, TILE), 0)
        ci = lax.broadcasted_iota(jnp.int32, (SUB, TILE), 1)
        a = [tile[SUB * i : SUB * i + SUB] for i in range(GROUPS)]
        e = [(ri + SUB * i == ci).astype(f32) for i in range(GROUPS)]
        inverse = factor_tile(a, e)
        between(k, 1)
        work[kb, window] = mm3(inverse, work[kb, window], ((1,), (0,)))

        @pl.loop(k + 1, STEPS)
        def _(i):
            ib = pl.ds(pl.multiple_of(i * TILE, TILE), TILE)
            work[ib, window] -= mm3(work[kb, ib], work[kb, window], ((0,), (0,)))


class Exchange:
    def __init__(self, send_sems, recv_sems):
        self.send_sems, self.recv_sems, self.used = send_sems, recv_sems, 0
        self.sent = []

    def copy(self, ref, out_at, in_at, device, sends=None, receives=None, source=None):
        n = self.used
        self.used += 1

        def made(at, src):
            return pltpu.make_async_remote_copy(
                src_ref=src,
                dst_ref=ref.at[at],
                send_sem=self.send_sems.at[n],
                recv_sem=self.recv_sems.at[n],
                device_id=device,
                device_id_type=pl.DeviceIdType.MESH,
            )

        def start():
            made(out_at, ref.at[out_at] if source is None else source).start()

        def wait_recv():
            made(in_at, ref.at[in_at]).wait_recv()

        def wait_send():
            made(out_at, ref.at[out_at] if source is None else source).wait_send()

        sent = (sends, wait_send)
        self.sent.append(sent)
        return (sends, start), (receives, wait_recv), sent

    def drain(self, copies=None):
        waits = self.sent if copies is None else [copy[2] for copy in copies]
        for guard, wait in waits:
            guarded(guard, wait)
        self.sent = [w for w in self.sent if not any(w is done for done in waits)]


def guarded(guard, action):
    if guard is None:
        action()
    else:
        pl.when(guard)(action)


def begin(copies):
    for (guard, start), _, _ in copies:
        guarded(guard, start)
    return copies


def finish(copies):
    for _, (guard, wait), _ in copies:
        guarded(guard, wait)


def relay(r, c, rows, cols, map_ref, child_ref, moved_ref, held, turned, sems):
    groups = 2 * 3
    me = r * cols + c
    group = (c + cols - 2 * r % cols) % cols
    holds = group < groups
    child, run = group // 3 % 2, group % 3
    count = rows * groups

    def column(k, g):
        return (g + 2 * k) % cols

    def rows_of(g, k):
        return pl.ds(pl.multiple_of(g % 3 * TILE + k * SUB, SUB), SUB)

    def first(k, g):
        return pltpu.make_async_remote_copy(
            src_ref=child_ref.at[g // 3, rows_of(g, k)],
            dst_ref=held.at[me],
            send_sem=sems.at[0],
            recv_sem=sems.at[1],
            device_id=(k, column(k, g)),
            device_id_type=pl.DeviceIdType.MESH,
        )

    def second(e):
        return pltpu.make_async_remote_copy(
            src_ref=turned.at[e],
            dst_ref=moved_ref.at[child, rows_of(group, r)],
            send_sem=sems.at[2],
            recv_sem=sems.at[3],
            device_id=(e // cols, e % cols),
            device_id_type=pl.DeviceIdType.MESH,
        )

    def all_of(ref, n):
        return ref.at[pl.ds(0, n)]

    def waiting(n, sem):
        return pltpu.make_async_copy(all_of(held, n), all_of(turned, n), sem)

    @pl.loop(0, count)
    def _(i):
        j = i * STRIDE1 % count
        k, g = (r + j // groups) % rows, (j + c) % groups

        @pl.when(k * cols + column(k, g) != me)
        def _():
            first(k, g).start()

    @pl.when(holds)
    def _():
        held[me] = child_ref[child, rows_of(group, r)]
        waiting(rows * cols - 1, sems.at[1]).wait()
        row_start = map_ref[child, run * RUN]
        col_starts = [map_ref[child, n * RUN] for n in range(3)]

        @pl.loop(0, rows * cols)
        def _(i):
            e = (me + i * STRIDE2) % (rows * cols)
            source = (e // cols + 2 * TILE - row_start) % rows * cols
            for n in range(3):
                part = slice(n * 2 * TILE, (n + 1) * 2 * TILE)
                turned[e, :, part] = held[source + (e % cols + 2 * TILE - col_starts[n]) % cols, :, part]

            @pl.when(i > 0)
            def _():
                second(e).start()

        moved_ref[child, rows_of(group, r)] = turned[me]
        waiting(count - 1, sems.at[0]).wait()
        waiting(rows * cols - 1, sems.at[2]).wait()
        waiting(count - 1, sems.at[3]).wait()

    @pl.when(group >= groups)
    def _():
        waiting(count, sems.at[0]).wait()
        waiting(count, sems.at[3]).wait()


def gather_kernel(
    map_ref, front_ref, child_ref, solved_out, uh_out, ul_out, bh_out, bl_out, moved_out,
    wrow_ref, uh_ref, ul_ref, bh_ref, bl_ref, moved_ref,
    strip_ref, cols_ref, xh_ref, xl_ref, wcol_ref, held, turned, pivots, work,
    strip_sems, out_sems, relay_sems, send_sems, recv_sems,
):
    rows, cols = lax.axis_size("row"), lax.axis_size("col")
    r, c = lax.axis_index("row"), lax.axis_index("col")
    x, yl, core = r // 4, r // 2 % 2, r % 2
    yh, z = c // 4, c % 4
    y = yh * 2 + yl
    at = {"x": x, "y": y, "z": z}
    near = x < 2
    xs = x % 2

    def device(x=x, y=y, z=z, core=core):
        return (x * 4 + y % 2 * 2 + core, y // 2 * 4 + z)

    def moved(dim, step):
        return (at[dim] + step) % 4

    strips = [
        pltpu.make_async_copy(front_ref.at[:, pl.ds(0, TILE)], strip_ref, strip_sems.at[0]),
        pltpu.make_async_copy(front_ref.at[pl.ds(0, TILE), :], cols_ref, strip_sems.at[1]),
    ]
    for copy in strips:
        copy.start()
    barrier = pltpu.get_barrier_semaphore()

    @pl.loop(1, rows * cols)
    def _(i):
        e = (r * cols + c + i) % (rows * cols)
        pl.semaphore_signal(barrier, inc=1, device_id=(e // cols, e % cols), device_id_type=pl.DeviceIdType.MESH)

    pl.semaphore_wait(barrier, rows * cols - 1)
    relay(r, c, rows, cols, map_ref, child_ref, moved_ref, held, turned, relay_sems)

    results = []

    def deliver(src, dst):
        copy = pltpu.make_async_copy(src, dst, out_sems.at[len(results)])
        copy.start()
        results.append(copy)

    deliver(moved_ref, moved_out)
    for copy in strips:
        copy.wait()

    def kept(condition, value):
        return jnp.where(condition, value, jnp.zeros_like(value))

    own_cols = pl.ds(pl.multiple_of(c * TILE, TILE), TILE)
    for slot in range(rows // 2):
        block = slice(slot * TILE, (slot + 1) * TILE)
        total = strip_ref[block, :]
        for child in range(2):
            inside = c >= map_ref[child, 0]
            for run in range(3):
                offset = slot * rows + r - map_ref[child, run * RUN]
                total = total + kept(
                    inside & (offset >= 0) & (offset < RUN), moved_ref[child, run * TILE : (run + 1) * TILE, :TILE]
                )
        wrow_ref[block, own_cols] = total

    @pl.when(near)
    def _():
        pivots[core, xs, y, z] = wrow_ref[:TILE, own_cols]
        for slot in range(2 * cols):
            block = slice(slot * TILE, (slot + 1) * TILE)
            total = cols_ref[:, block]
            for child in range(2):
                inside = r >= map_ref[child, 0]
                for tile in range(6):
                    offset = slot * cols + c - map_ref[child, tile // 2 * RUN] - tile % 2 * cols
                    total = total + kept(
                        inside & (offset >= 0) & (offset < cols),
                        moved_ref[child, :TILE, tile * TILE : (tile + 1) * TILE],
                    )
            wcol_ref[r % 8, :, block] = total

    ex = Exchange(send_sems, recv_sems)

    def pivot_phase(rows, order, number):
        dim, done = order[number], order[:number]
        waits = []
        for step in range(1, 4):

            def block(**over):
                place = {"x": xs, "y": y, "z": z, **over}
                full = {"x": pl.ds(0, 2), "y": pl.ds(0, 4), "z": pl.ds(0, 4)}
                index = [full[d] if d in done else place[d] for d in "xyz"]
                return (core, *index, pl.ds(rows[0], rows[1] - rows[0]))

            source = moved(dim, -step)
            if "x" in done:
                sends = receives = None
            elif dim == "x":
                sends, receives = near, source < 2
            else:
                sends = receives = near
            waits.append(
                ex.copy(
                    pivots,
                    block(),
                    block(**{dim: source % 2 if dim == "x" else source}),
                    device(**{dim: moved(dim, step)}),
                    sends,
                    receives,
                )
            )
        return begin(waits)

    def pivot_swap(rows):
        def block(k):
            full = (pl.ds(0, 2), pl.ds(0, 4), pl.ds(0, 4))
            return (k, *full, pl.ds(rows[0], rows[1] - rows[0]))

        return begin([ex.copy(pivots, block(core), block(1 - core), device(core=1 - core))])

    def tiles(first, count):
        return pl.ds(pl.multiple_of(first * TILE, TILE), count * TILE)

    def panel_row(rows, first, count, first_in, device):
        return ex.copy(wrow_ref, (rows, tiles(first, count)), (rows, tiles(first_in, count)), device)

    def panel_col(chunk, out, into, device, sends=None, receives=None):
        return ex.copy(
            wcol_ref, (out, pl.ds(0, TILE), chunk), (into, pl.ds(0, TILE), chunk), device, sends, receives
        )

    def owner(x, yl, core=core):
        return x * 4 + yl * 2 + core

    y_far = device(y=(y + 2) % 4)
    y_pair = device(y=yh * 2 + 1 - yl)
    x_pair = device(x=(5 - x) % 4)
    sibling = device(core=1 - core)
    top, bottom = pl.ds(0, ROW_SPLIT), pl.ds(ROW_SPLIT, strip_ref.shape[0] - ROW_SPLIT)
    top_first = [panel_row(top, c, 1, (c + cols // 2) % cols, y_far)]
    bottom_first = [
        panel_row(bottom, c, 1, yh * 4 + moved("z", -step), device(z=moved("z", step))) for step in range(1, 4)
    ]
    top_last = [
        panel_row(top, h * 4 + z, 1, h * 4 + moved("z", -step), device(z=moved("z", step)))
        for step in (1, 3, 2)
        for h in range(2)
    ]
    bottom_last = [panel_row(bottom, yh * 4, 4, (1 - yh) * 4, y_far)]

    def beside(chunk, halves):
        return [
            panel_col(
                chunk,
                owner(xs, h),
                owner(moved("x", -step) % 2, h),
                device(x=moved("x", step)),
                near,
                moved("x", -step) < 2,
            )
            for step in (1, 3)
            for h in halves
        ]

    def onward(chunk, halves):
        far = x >= 2
        return [panel_col(chunk, owner((x + 1) % 2, h), owner(xs, h), x_pair, far, far) for h in halves]

    def swapped(chunk):
        return [
            panel_col(chunk, owner(a, b), owner(a, b, 1 - core), sibling) for a in range(2) for b in range(2)
        ]

    chunks = [pl.ds(TILE + n * 5 * TILE, 5 * TILE) for n in range(3)]
    both = (0, 1)
    a_x, a_on = beside(chunks[0], (yl,)), onward(chunks[0], (yl,))
    a_y = [panel_col(chunks[0], owner(h, yl), owner(h, 1 - yl), y_pair) for h in both]
    b_y, c_y = ([panel_col(chunks[n], owner(xs, yl), owner(xs, 1 - yl), y_pair, near, near)] for n in (1, 2))
    b_x, c_x = (beside(chunks[n], both) for n in (1, 2))
    b_on, c_on = (onward(chunks[n], both) for n in (1, 2))
    swaps = [swapped(chunk) for chunk in chunks]

    parts = (((0, 48), "xyz"), ((48, 96), "zxy"), ((96, 128), "yzx"))
    pending = [pivot_phase(rows, order, 0) for rows, order in parts]
    for number in (1, 2):
        for p, (rows, order) in enumerate(parts):
            finish(pending[p])
            pending[p] = pivot_phase(rows, order, number)
        if number == EARLY:
            for copies in (a_x, b_y, bottom_first, top_first, c_y):
                begin(copies)
    for p, (rows, order) in enumerate(parts):
        finish(pending[p])
        pending[p] = pivot_swap(rows)
    for p in range(3):
        finish(pending[p])
    load_block(pivots, work)

    def then(before, after):
        finish(before)
        begin(after)

    plan = {
        (0, 0): [(a_x, a_on), (b_y, b_x)],
        (0, 1): [(top_first, top_last)],
        (1, 1): [(a_on, a_y), (bottom_first, bottom_last)],
        (2, 0): [(c_y, c_x)],
        (2, 1): [(b_x, b_on)],
        (5, 0): [(c_x, c_on), (b_on, swaps[1])],
        (4, 1): [(a_y, swaps[0])],
    }

    def between(k, place):
        for (step, at_place), pairs in plan.items():
            if at_place == place:

                @pl.when(k == step)
                def _():
                    for before, after in pairs:
                        then(before, after)

    factor_steps(work, between)
    for i in range(STEPS):
        block = slice(i * TILE, (i + 1) * TILE)
        xh_ref[block], xl_ref[block] = split2(work[block, PIVOTS:])
    for copies in (top_first, top_last, bottom_first, bottom_last):
        if copies in (top_last, bottom_last):
            finish(copies)
        ex.drain(copies)
    solve_rows(lax.axis_size("row"), r, xh_ref, xl_ref, wrow_ref, uh_ref, ul_ref)
    deliver(wrow_ref, solved_out)
    deliver(uh_ref, uh_out)
    deliver(ul_ref, ul_out)
    then(c_on, swaps[2])
    bh_ref[:, :TILE] = jnp.zeros((PIVOTS, TILE), bf16)
    bl_ref[:, :TILE] = jnp.zeros((PIVOTS, TILE), bf16)
    for n in range(3):
        finish(swaps[n])
        first, last = TILE + n * 5 * TILE, TILE + (n + 1) * 5 * TILE
        solve_cols(slice(first, last), xh_ref, xl_ref, wcol_ref, bh_ref, bl_ref)
        done = pl.ds(first, last - first) if n else pl.ds(0, last)
        deliver(bh_ref.at[:, done], bh_out.at[:, done])
        deliver(bl_ref.at[:, done], bl_out.at[:, done])
    ex.drain()
    for copy in results:
        copy.wait()


def dot3(ah, al, bh, bl, dims):
    def dot(p, q):
        return lax.dot_general(p, q, (dims, ((), ())), preferred_element_type=f32)

    return dot(ah, bh) + (dot(ah, bl) + dot(al, bh))


QUARTER = 256


def solve_rows(rows, r, xh_ref, xl_ref, wrow_ref, uh_ref, ul_ref):
    @pl.loop(0, wrow_ref.shape[0] // QUARTER)
    def _(i):
        block = pl.ds(pl.multiple_of(i * QUARTER, QUARTER), QUARTER)
        wh, wl = split2(wrow_ref[block, :])
        slot = lax.broadcasted_iota(jnp.int32, (QUARTER, QUARTER), 0) // TILE + i * (QUARTER // TILE)
        pivot = slot * rows + r < STEPS
        for n in range(PIVOTS // QUARTER):
            part = slice(n * QUARTER, (n + 1) * QUARTER)
            depth = slice(0, (n + 1) * QUARTER)
            b = dot3(wh[:, depth], wl[:, depth], xh_ref[part, depth], xl_ref[part, depth], ((1,), (1,)))
            wrow_ref[block, part] = b
            uh_ref[block, part], ul_ref[block, part] = split2(jnp.where(pivot, 0.0, b))


def solve_cols(chunk, xh_ref, xl_ref, wcol_ref, bh_ref, bl_ref):
    wh, wl = split2(wcol_ref[:, :, chunk].reshape(PIVOTS, chunk.stop - chunk.start))
    for n in range(PIVOTS // QUARTER):
        part = slice(n * QUARTER, (n + 1) * QUARTER)
        depth = slice(0, (n + 1) * QUARTER)
        b = dot3(xh_ref[part, depth], xl_ref[part, depth], wh[depth], wl[depth], ((1,), (0,)))
        bh_ref[part, chunk], bl_ref[part, chunk] = split2(b)


ROW_SPLIT = 768
EARLY = 2
COPIES = 80


def gather_and_factor(child_map, front, children):
    vmem = pl.BlockSpec(memory_space=pltpu.VMEM)
    local_rows, local_cols = front.shape
    slices = (lax.axis_size("row") * lax.axis_size("col"), SUB, children.shape[2])
    row_half = jax.ShapeDtypeStruct((local_rows, PIVOTS), bf16)
    col_half = jax.ShapeDtypeStruct((PIVOTS, local_cols), bf16)
    return pl.pallas_call(
        gather_kernel,
        out_shape=(
            jax.ShapeDtypeStruct((local_rows, PIVOTS), f32),
            row_half,
            row_half,
            col_half,
            col_half,
            jax.ShapeDtypeStruct(children.shape, f32),
        ),
        in_specs=[pl.BlockSpec(memory_space=pltpu.SMEM), pl.BlockSpec(memory_space=pl.ANY), vmem],
        out_specs=(pl.BlockSpec(memory_space=pl.ANY),) * 6,
        scratch_shapes=[
            pltpu.VMEM((local_rows, PIVOTS), f32),
            pltpu.VMEM(row_half.shape, bf16),
            pltpu.VMEM(row_half.shape, bf16),
            pltpu.VMEM(col_half.shape, bf16),
            pltpu.VMEM(col_half.shape, bf16),
            pltpu.VMEM(children.shape, f32),
            pltpu.VMEM((local_rows, TILE), f32),
            pltpu.VMEM((TILE, local_cols), f32),
            pltpu.VMEM((PIVOTS, PIVOTS), bf16),
            pltpu.VMEM((PIVOTS, PIVOTS), bf16),
            pltpu.VMEM((STEPS, TILE, local_cols), f32),
            pltpu.VMEM(slices, f32),
            pltpu.VMEM(slices, f32),
            pltpu.VMEM((2, 2, 4, 4, TILE, TILE), f32),
            pltpu.VMEM((PIVOTS, 2 * PIVOTS), f32),
            pltpu.SemaphoreType.DMA((2,)),
            pltpu.SemaphoreType.DMA((10,)),
            pltpu.SemaphoreType.DMA((4,)),
            pltpu.SemaphoreType.DMA((COPIES,)),
            pltpu.SemaphoreType.DMA((COPIES,)),
        ],
        compiler_params=pltpu.CompilerParams(
            vmem_limit_bytes=60 * MIB, collective_id=0, has_side_effects=True
        ),
        cost_estimate=pl.CostEstimate(flops=5 * 10**10, bytes_accessed=8 * MIB, transcendentals=0),
        name="gather_factor",
    )(child_map, front, children)


def update_kernel(slots_ref, front_ref, moved_ref, solved_ref, uh_ref, ul_ref, bh_ref, bl_ref, out_ref, lower_ref):
    step = pl.program_id(0)
    row = lax.broadcasted_iota(jnp.int32, solved_ref.shape, 0) + slots_ref[2, step] * TILE
    col = lax.broadcasted_iota(jnp.int32, solved_ref.shape, 1)
    lower_ref[...] = jnp.where(row >= col, solved_ref[...], 0.0)
    for n in range(front_ref.shape[0] // QUARTER):
        block = slice(n * QUARTER, (n + 1) * QUARTER)
        out_ref[block] = front_ref[block] - dot3(uh_ref[block], ul_ref[block], bh_ref[...], bl_ref[...], ((1,), (0,)))
    for child in range(2):
        for tile in range(6):
            slot = slots_ref[1, child * 6 + tile]

            @pl.when(slot // (QUARTER // TILE) == step)
            def _():
                col = pl.ds(pl.multiple_of(slot % (QUARTER // TILE) * TILE, TILE), TILE)
                for run in range(3):
                    row = pl.ds(pl.multiple_of(slots_ref[0, child * 3 + run] * TILE, TILE), TILE)
                    out_ref[row, col] += moved_ref[child, run * TILE : (run + 1) * TILE, tile * TILE : (tile + 1) * TILE]


def update(slots, front, moved, solved, uh, ul, bh, bl):
    rows, cols = front.shape
    rows_whole = pl.BlockSpec((rows, PIVOTS), lambda j: (0, 0), pipeline_mode=pl.Buffered(1))
    block = pl.BlockSpec((rows, QUARTER), lambda j: (0, j))
    cols_block = pl.BlockSpec((PIVOTS, QUARTER), lambda j: (0, j))
    lower_block = pl.BlockSpec((rows // (cols // QUARTER), PIVOTS), lambda j: (j, 0))
    return pl.pallas_call(
        update_kernel,
        grid=(cols // QUARTER,),
        out_shape=(jax.ShapeDtypeStruct(front.shape, f32), jax.ShapeDtypeStruct(solved.shape, f32)),
        in_specs=[
            pl.BlockSpec(memory_space=pltpu.SMEM),
            block,
            pl.BlockSpec(moved.shape, lambda j: (0, 0, 0), pipeline_mode=pl.Buffered(1)),
            lower_block,
            rows_whole,
            rows_whole,
            cols_block,
            cols_block,
        ],
        out_specs=(block, lower_block),
        compiler_params=pltpu.CompilerParams(vmem_limit_bytes=60 * MIB),
        name="update",
    )(slots, front, moved, solved, uh, ul, bh, bl)


def per_device(front, children, child_map):
    rows, cols = lax.axis_size("row"), lax.axis_size("col")
    row_index, col_index = lax.axis_index("row"), lax.axis_index("col")
    solved, uh, ul, bh, bl, moved = gather_and_factor(child_map, front, children)
    starts = child_map[:, ::RUN]
    row_slots = (starts + (row_index - starts) % rows) // rows
    col_slots = (starts + (col_index - starts) % cols) // cols
    col_slots = col_slots[:, :, None] + jnp.arange(RUN // cols)[None, None, :]
    slots = jnp.zeros((3, 12), jnp.int32).at[0, :6].set(row_slots.reshape(-1)).at[1].set(col_slots.reshape(-1))
    slots = slots.at[2].set(jnp.arange(12) * rows + row_index)
    return update(slots, front, moved, solved, uh, ul, bh, bl)


def solution(mesh):
    return jax.shard_map(
        per_device,
        mesh=mesh,
        in_specs=(P("row", "col"), P(None, "row", "col"), P()),
        out_specs=(P("row", "col"), P("row", None)),
        check_vma=False,
    )
```

```python
import jax
import jax.numpy as jnp
from jax import lax
from jax.experimental import pallas as pl
from jax.experimental.pallas import tpu as pltpu
from jax.sharding import PartitionSpec as P

f32 = jnp.float32
bf16 = jnp.bfloat16
TILE = 128
RUN = 16
PIVOTS = 1024
STEPS = PIVOTS // TILE
SUB = 8
STRIDE1 = 29
STRIDE2 = 37
GROUPS = TILE // SUB
MIB = 2**20


def split2(x):
    hi = x.astype(bf16)
    return hi, (x - hi.astype(f32)).astype(bf16)


def split3(x):
    hi = x.astype(bf16).astype(f32)
    rest = x - hi
    mid = rest.astype(bf16).astype(f32)
    return hi, mid, rest - mid


def stacked_dot(a, b, dim):
    return lax.dot_general(a, b, (((dim,), (0,)), ((), ())), preferred_element_type=f32)


def lane(x, k):
    return jnp.broadcast_to(x[:, k : k + 1], (SUB, TILE))


def sublane(x, k):
    return jnp.broadcast_to(x[k : k + 1, :], (SUB, TILE))


def factor_tile(a, e):
    row_of = lax.broadcasted_iota(jnp.int32, (SUB, TILE), 0)

    def packed(v):
        out = v[SUB - 1]
        for t in range(SUB - 2, -1, -1):
            out = jnp.where(row_of == t, v[t], out)
        return out

    inverse_rows = []
    last_u = last_e = None
    for b in range(GROUPS):
        r = [sublane(a[b], t) for t in range(SUB)]
        w = [sublane(e[b], t) for t in range(SUB)]
        if b:
            for s in range(SUB):
                for t in range(SUB):
                    factor = lane(last_u[t], SUB * b + s)
                    r[s] = r[s] - factor * last_u[t]
                    w[s] = w[s] - factor * last_e[t]
        d = [[lane(r[t], SUB * b + s) if s >= t else None for t in range(SUB)] for s in range(SUB)]
        u = [None] * SUB
        v = [None] * SUB
        for t in range(SUB):
            scale = lax.rsqrt(d[t][t])
            u[t] = r[t] * scale
            v[t] = w[t] * scale
            below = [d[s][t] * scale if s > t else None for s in range(SUB)]
            for s in range(t + 1, SUB):
                for q in range(t + 1, s + 1):
                    d[s][q] = d[s][q] - below[s] * below[q]
            for s in range(t + 1, SUB):
                r[s] = r[s] - below[s] * u[t]
                w[s] = w[s] - below[s] * v[t]
        last_u, last_e = u, v
        urows, erows = packed(u), packed(v)
        inverse_rows.append(erows)
        if b < GROUPS - 2:
            uh, um, ul = split3(urows)
            eh, em, el = split3(erows)
            left = jnp.concatenate([uh, uh, um, um, uh, ul], 0).astype(bf16)
            right = jnp.concatenate(
                [jnp.concatenate([uh, um, uh, um, ul, uh], 0), jnp.concatenate([eh, em, eh, em, el, eh], 0)], 1
            ).astype(bf16)
            change = lax.dot_general(left, right, (((0,), (0,)), ((), ())), preferred_element_type=f32)
            for i in range(b + 2, GROUPS):
                a[i] = a[i] - change[SUB * i : SUB * i + SUB, :TILE]
                e[i] = e[i] - change[SUB * i : SUB * i + SUB, TILE:]
    return jnp.concatenate(inverse_rows, 0)


def load_block(pivots, work):
    for x in range(2):
        for y in range(4):
            for z in range(4):
                for core in range(2):
                    i = x * 4 + y % 2 * 2 + core
                    j = y // 2 * 4 + z
                    work[i * TILE : (i + 1) * TILE, j * TILE : (j + 1) * TILE] = pivots[core, x, y, z]
    for i in range(STEPS):
        ri = lax.broadcasted_iota(jnp.int32, (TILE, PIVOTS), 0) + i * TILE
        ci = lax.broadcasted_iota(jnp.int32, (TILE, PIVOTS), 1)
        work[i * TILE : (i + 1) * TILE, PIVOTS:] = (ri == ci).astype(f32)


def factor_steps(work, left_ref, right_ref, between):
    width = (STEPS + 1) * TILE

    @pl.loop(0, STEPS)
    def _(k):
        between(k, 0)
        kb = pl.ds(pl.multiple_of(k * TILE, TILE), TILE)
        window = pl.ds(pl.multiple_of(k * TILE, TILE), width)
        tile = work[kb, kb]
        ri = lax.broadcasted_iota(jnp.int32, (SUB, TILE), 0)
        ci = lax.broadcasted_iota(jnp.int32, (SUB, TILE), 1)
        a = [tile[SUB * i : SUB * i + SUB] for i in range(GROUPS)]
        e = [(ri + SUB * i == ci).astype(f32) for i in range(GROUPS)]
        inverse = factor_tile(a, e)
        between(k, 1)
        lh, ll = split2(inverse)
        wh, wl = split2(work[kb, window])
        solved = stacked_dot(jnp.concatenate([lh, lh, ll], 1), jnp.concatenate([wh, wl, wh], 0), 1)
        work[kb, window] = solved
        ph, pl_ = split2(solved)
        for n, (a_part, b_part) in enumerate(((ph, ph), (ph, pl_), (pl_, ph))):
            left_ref[n * TILE : (n + 1) * TILE] = a_part
            right_ref[n * TILE : (n + 1) * TILE] = b_part

        @pl.loop(k + 1, STEPS)
        def _(i):
            ib = pl.ds(pl.multiple_of(i * TILE, TILE), TILE)
            own = pl.ds(pl.multiple_of((i - k) * TILE, TILE), TILE)
            work[ib, window] -= stacked_dot(left_ref[:, own], right_ref[...], 0)


class Exchange:
    def __init__(self, send_sems, recv_sems):
        self.send_sems, self.recv_sems, self.used = send_sems, recv_sems, 0
        self.sent = []

    def copy(self, ref, out_at, in_at, device, sends=None, receives=None, source=None):
        n = self.used
        self.used += 1

        def made(at, src):
            return pltpu.make_async_remote_copy(
                src_ref=src,
                dst_ref=ref.at[at],
                send_sem=self.send_sems.at[n],
                recv_sem=self.recv_sems.at[n],
                device_id=device,
                device_id_type=pl.DeviceIdType.MESH,
            )

        def start():
            made(out_at, ref.at[out_at] if source is None else source).start()

        def wait_recv():
            made(in_at, ref.at[in_at]).wait_recv()

        def wait_send():
            made(out_at, ref.at[out_at] if source is None else source).wait_send()

        sent = (sends, wait_send)
        self.sent.append(sent)
        return (sends, start), (receives, wait_recv), sent

    def drain(self, copies=None):
        waits = self.sent if copies is None else [copy[2] for copy in copies]
        for guard, wait in waits:
            guarded(guard, wait)
        self.sent = [w for w in self.sent if not any(w is done for done in waits)]


def guarded(guard, action):
    if guard is None:
        action()
    else:
        pl.when(guard)(action)


def begin(copies):
    for (guard, start), _, _ in copies:
        guarded(guard, start)
    return copies


def finish(copies):
    for _, (guard, wait), _ in copies:
        guarded(guard, wait)


def relay(r, c, rows, cols, map_ref, child_ref, moved_ref, held, turned, sems):
    groups = 2 * 3
    me = r * cols + c
    group = (c + cols - 2 * r % cols) % cols
    holds = group < groups
    child, run = group // 3 % 2, group % 3
    count = rows * groups

    def column(k, g):
        return (g + 2 * k) % cols

    def rows_of(g, k):
        return pl.ds(pl.multiple_of(g % 3 * TILE + k * SUB, SUB), SUB)

    def first(k, g):
        return pltpu.make_async_remote_copy(
            src_ref=child_ref.at[g // 3, rows_of(g, k)],
            dst_ref=held.at[me],
            send_sem=sems.at[0],
            recv_sem=sems.at[1],
            device_id=(k, column(k, g)),
            device_id_type=pl.DeviceIdType.MESH,
        )

    def second(e):
        return pltpu.make_async_remote_copy(
            src_ref=turned.at[e],
            dst_ref=moved_ref.at[child, rows_of(group, r)],
            send_sem=sems.at[2],
            recv_sem=sems.at[3],
            device_id=(e // cols, e % cols),
            device_id_type=pl.DeviceIdType.MESH,
        )

    def all_of(ref, n):
        return ref.at[pl.ds(0, n)]

    def waiting(n, sem):
        return pltpu.make_async_copy(all_of(held, n), all_of(turned, n), sem)

    @pl.loop(0, count)
    def _(i):
        j = i * STRIDE1 % count
        k, g = (r + j // groups) % rows, (j + c) % groups

        @pl.when(k * cols + column(k, g) != me)
        def _():
            first(k, g).start()

    @pl.when(holds)
    def _():
        held[me] = child_ref[child, rows_of(group, r)]
        waiting(rows * cols - 1, sems.at[1]).wait()
        row_start = map_ref[child, run * RUN]
        col_starts = [map_ref[child, n * RUN] for n in range(3)]

        @pl.loop(0, rows * cols)
        def _(i):
            e = (me + i * STRIDE2) % (rows * cols)
            source = (e // cols + 2 * TILE - row_start) % rows * cols
            for n in range(3):
                part = slice(n * 2 * TILE, (n + 1) * 2 * TILE)
                turned[e, :, part] = held[source + (e % cols + 2 * TILE - col_starts[n]) % cols, :, part]

            @pl.when(i > 0)
            def _():
                second(e).start()

        moved_ref[child, rows_of(group, r)] = turned[me]
        waiting(count - 1, sems.at[0]).wait()
        waiting(rows * cols - 1, sems.at[2]).wait()
        waiting(count - 1, sems.at[3]).wait()

    @pl.when(group >= groups)
    def _():
        waiting(count, sems.at[0]).wait()
        waiting(count, sems.at[3]).wait()


def gather_kernel(
    map_ref, front_ref, child_ref, solved_out, uh_out, ul_out, bh_out, bl_out, moved_out,
    wrow_ref, uh_ref, ul_ref, bh_ref, bl_ref, moved_ref,
    strip_ref, cols_ref, xh_ref, xl_ref, wcol_ref, held, turned, pivots, work, left_ref, right_ref,
    strip_sems, out_sems, relay_sems, send_sems, recv_sems,
):
    rows, cols = lax.axis_size("row"), lax.axis_size("col")
    r, c = lax.axis_index("row"), lax.axis_index("col")
    x, yl, core = r // 4, r // 2 % 2, r % 2
    yh, z = c // 4, c % 4
    y = yh * 2 + yl
    at = {"x": x, "y": y, "z": z}
    near = x < 2
    xs = x % 2

    def device(x=x, y=y, z=z, core=core):
        return (x * 4 + y % 2 * 2 + core, y // 2 * 4 + z)

    def moved(dim, step):
        return (at[dim] + step) % 4

    strips = [
        pltpu.make_async_copy(front_ref.at[:, pl.ds(0, TILE)], strip_ref, strip_sems.at[0]),
        pltpu.make_async_copy(front_ref.at[pl.ds(0, TILE), :], cols_ref, strip_sems.at[1]),
    ]
    for copy in strips:
        copy.start()
    barrier = pltpu.get_barrier_semaphore()

    @pl.loop(1, rows * cols)
    def _(i):
        e = (r * cols + c + i) % (rows * cols)
        pl.semaphore_signal(barrier, inc=1, device_id=(e // cols, e % cols), device_id_type=pl.DeviceIdType.MESH)

    pl.semaphore_wait(barrier, rows * cols - 1)
    relay(r, c, rows, cols, map_ref, child_ref, moved_ref, held, turned, relay_sems)

    results = []

    def deliver(src, dst):
        copy = pltpu.make_async_copy(src, dst, out_sems.at[len(results)])
        copy.start()
        results.append(copy)

    deliver(moved_ref, moved_out)
    for copy in strips:
        copy.wait()

    def kept(condition, value):
        return jnp.where(condition, value, jnp.zeros_like(value))

    own_cols = pl.ds(pl.multiple_of(c * TILE, TILE), TILE)
    for slot in range(rows // 2):
        block = slice(slot * TILE, (slot + 1) * TILE)
        total = strip_ref[block, :]
        for child in range(2):
            inside = c >= map_ref[child, 0]
            for run in range(3):
                offset = slot * rows + r - map_ref[child, run * RUN]
                total = total + kept(
                    inside & (offset >= 0) & (offset < RUN), moved_ref[child, run * TILE : (run + 1) * TILE, :TILE]
                )
        wrow_ref[block, own_cols] = total

    @pl.when(near)
    def _():
        pivots[core, xs, y, z] = wrow_ref[:TILE, own_cols]
        for slot in range(2 * cols):
            block = slice(slot * TILE, (slot + 1) * TILE)
            total = cols_ref[:, block]
            for child in range(2):
                inside = r >= map_ref[child, 0]
                for tile in range(6):
                    offset = slot * cols + c - map_ref[child, tile // 2 * RUN] - tile % 2 * cols
                    total = total + kept(
                        inside & (offset >= 0) & (offset < cols),
                        moved_ref[child, :TILE, tile * TILE : (tile + 1) * TILE],
                    )
            wcol_ref[r % 8, :, block] = total

    ex = Exchange(send_sems, recv_sems)

    def pivot_phase(rows, order, number):
        dim, done = order[number], order[:number]
        waits = []
        for step in range(1, 4):

            def block(**over):
                place = {"x": xs, "y": y, "z": z, **over}
                full = {"x": pl.ds(0, 2), "y": pl.ds(0, 4), "z": pl.ds(0, 4)}
                index = [full[d] if d in done else place[d] for d in "xyz"]
                return (core, *index, pl.ds(rows[0], rows[1] - rows[0]))

            source = moved(dim, -step)
            if "x" in done:
                sends = receives = None
            elif dim == "x":
                sends, receives = near, source < 2
            else:
                sends = receives = near
            waits.append(
                ex.copy(
                    pivots,
                    block(),
                    block(**{dim: source % 2 if dim == "x" else source}),
                    device(**{dim: moved(dim, step)}),
                    sends,
                    receives,
                )
            )
        return begin(waits)

    def pivot_swap(rows):
        def block(k):
            full = (pl.ds(0, 2), pl.ds(0, 4), pl.ds(0, 4))
            return (k, *full, pl.ds(rows[0], rows[1] - rows[0]))

        return begin([ex.copy(pivots, block(core), block(1 - core), device(core=1 - core))])

    def tiles(first, count):
        return pl.ds(pl.multiple_of(first * TILE, TILE), count * TILE)

    def panel_row(rows, first, count, first_in, device):
        return ex.copy(wrow_ref, (rows, tiles(first, count)), (rows, tiles(first_in, count)), device)

    def panel_col(chunk, out, into, device, sends=None, receives=None):
        return ex.copy(
            wcol_ref, (out, pl.ds(0, TILE), chunk), (into, pl.ds(0, TILE), chunk), device, sends, receives
        )

    def owner(x, yl, core=core):
        return x * 4 + yl * 2 + core

    y_far = device(y=(y + 2) % 4)
    y_pair = device(y=yh * 2 + 1 - yl)
    x_pair = device(x=(5 - x) % 4)
    sibling = device(core=1 - core)
    top, bottom = pl.ds(0, ROW_SPLIT), pl.ds(ROW_SPLIT, strip_ref.shape[0] - ROW_SPLIT)
    top_first = [panel_row(top, c, 1, (c + cols // 2) % cols, y_far)]
    bottom_first = [
        panel_row(bottom, c, 1, yh * 4 + moved("z", -step), device(z=moved("z", step))) for step in range(1, 4)
    ]
    top_last = [
        panel_row(top, h * 4 + z, 1, h * 4 + moved("z", -step), device(z=moved("z", step)))
        for step in (1, 3, 2)
        for h in range(2)
    ]
    bottom_last = [panel_row(bottom, yh * 4, 4, (1 - yh) * 4, y_far)]

    def beside(chunk, halves):
        return [
            panel_col(
                chunk,
                owner(xs, h),
                owner(moved("x", -step) % 2, h),
                device(x=moved("x", step)),
                near,
                moved("x", -step) < 2,
            )
            for step in (1, 3)
            for h in halves
        ]

    def onward(chunk, halves):
        far = x >= 2
        return [panel_col(chunk, owner((x + 1) % 2, h), owner(xs, h), x_pair, far, far) for h in halves]

    def swapped(chunk):
        return [
            panel_col(chunk, owner(a, b), owner(a, b, 1 - core), sibling) for a in range(2) for b in range(2)
        ]

    chunks = [pl.ds(TILE + n * 5 * TILE, 5 * TILE) for n in range(3)]
    both = (0, 1)
    a_x, a_on = beside(chunks[0], (yl,)), onward(chunks[0], (yl,))
    a_y = [panel_col(chunks[0], owner(h, yl), owner(h, 1 - yl), y_pair) for h in both]
    b_y, c_y = ([panel_col(chunks[n], owner(xs, yl), owner(xs, 1 - yl), y_pair, near, near)] for n in (1, 2))
    b_x, c_x = (beside(chunks[n], both) for n in (1, 2))
    b_on, c_on = (onward(chunks[n], both) for n in (1, 2))
    swaps = [swapped(chunk) for chunk in chunks]

    parts = (((0, 48), "xyz"), ((48, 96), "zxy"), ((96, 128), "yzx"))
    pending = [pivot_phase(rows, order, 0) for rows, order in parts]
    for number in (1, 2):
        for p, (rows, order) in enumerate(parts):
            finish(pending[p])
            pending[p] = pivot_phase(rows, order, number)
        if number == EARLY:
            for copies in (a_x, b_y, bottom_first, top_first, c_y):
                begin(copies)
    for p, (rows, order) in enumerate(parts):
        finish(pending[p])
        pending[p] = pivot_swap(rows)
    for p in range(3):
        finish(pending[p])
    load_block(pivots, work)

    def then(before, after):
        finish(before)
        begin(after)

    plan = {
        (0, 0): [(a_x, a_on), (b_y, b_x)],
        (0, 1): [(top_first, top_last)],
        (1, 1): [(a_on, a_y), (bottom_first, bottom_last)],
        (2, 0): [(c_y, c_x)],
        (2, 1): [(b_x, b_on)],
        (5, 0): [(c_x, c_on), (b_on, swaps[1])],
        (4, 1): [(a_y, swaps[0])],
    }

    def between(k, place):
        for (step, at_place), pairs in plan.items():
            if at_place == place:

                @pl.when(k == step)
                def _():
                    for before, after in pairs:
                        then(before, after)

    factor_steps(work, left_ref, right_ref, between)
    for i in range(STEPS):
        block = slice(i * TILE, (i + 1) * TILE)
        xh_ref[block], xl_ref[block] = split2(work[block, PIVOTS:])
    for copies in (top_first, top_last, bottom_first, bottom_last):
        if copies in (top_last, bottom_last):
            finish(copies)
        ex.drain(copies)
    solve_rows(lax.axis_size("row"), r, xh_ref, xl_ref, wrow_ref, uh_ref, ul_ref)
    deliver(wrow_ref, solved_out)
    deliver(uh_ref, uh_out)
    deliver(ul_ref, ul_out)
    then(c_on, swaps[2])
    bh_ref[:, :TILE] = jnp.zeros((PIVOTS, TILE), bf16)
    bl_ref[:, :TILE] = jnp.zeros((PIVOTS, TILE), bf16)
    for n in range(3):
        finish(swaps[n])
        first, last = TILE + n * 5 * TILE, TILE + (n + 1) * 5 * TILE
        solve_cols(slice(first, last), xh_ref, xl_ref, wcol_ref, bh_ref, bl_ref)
        done = pl.ds(first, last - first) if n else pl.ds(0, last)
        deliver(bh_ref.at[:, done], bh_out.at[:, done])
        deliver(bl_ref.at[:, done], bl_out.at[:, done])
    ex.drain()
    for copy in results:
        copy.wait()


def dot3(ah, al, bh, bl, dims):
    def dot(p, q):
        return lax.dot_general(p, q, (dims, ((), ())), preferred_element_type=f32)

    return dot(ah, bh) + (dot(ah, bl) + dot(al, bh))


QUARTER = 256


def solve_rows(rows, r, xh_ref, xl_ref, wrow_ref, uh_ref, ul_ref):
    @pl.loop(0, wrow_ref.shape[0] // QUARTER)
    def _(i):
        block = pl.ds(pl.multiple_of(i * QUARTER, QUARTER), QUARTER)
        wh, wl = split2(wrow_ref[block, :])
        slot = lax.broadcasted_iota(jnp.int32, (QUARTER, QUARTER), 0) // TILE + i * (QUARTER // TILE)
        pivot = slot * rows + r < STEPS
        for n in range(PIVOTS // QUARTER):
            part = slice(n * QUARTER, (n + 1) * QUARTER)
            depth = slice(0, (n + 1) * QUARTER)
            b = dot3(wh[:, depth], wl[:, depth], xh_ref[part, depth], xl_ref[part, depth], ((1,), (1,)))
            wrow_ref[block, part] = b
            uh_ref[block, part], ul_ref[block, part] = split2(jnp.where(pivot, 0.0, b))


def solve_cols(chunk, xh_ref, xl_ref, wcol_ref, bh_ref, bl_ref):
    wh, wl = split2(wcol_ref[:, :, chunk].reshape(PIVOTS, chunk.stop - chunk.start))
    for n in range(PIVOTS // QUARTER):
        part = slice(n * QUARTER, (n + 1) * QUARTER)
        depth = slice(0, (n + 1) * QUARTER)
        b = dot3(xh_ref[part, depth], xl_ref[part, depth], wh[depth], wl[depth], ((1,), (0,)))
        bh_ref[part, chunk], bl_ref[part, chunk] = split2(b)


ROW_SPLIT = 768
EARLY = 2
COPIES = 80


def gather_and_factor(child_map, front, children):
    vmem = pl.BlockSpec(memory_space=pltpu.VMEM)
    local_rows, local_cols = front.shape
    slices = (lax.axis_size("row") * lax.axis_size("col"), SUB, children.shape[2])
    row_half = jax.ShapeDtypeStruct((local_rows, PIVOTS), bf16)
    col_half = jax.ShapeDtypeStruct((PIVOTS, local_cols), bf16)
    return pl.pallas_call(
        gather_kernel,
        out_shape=(
            jax.ShapeDtypeStruct((local_rows, PIVOTS), f32),
            row_half,
            row_half,
            col_half,
            col_half,
            jax.ShapeDtypeStruct(children.shape, f32),
        ),
        in_specs=[pl.BlockSpec(memory_space=pltpu.SMEM), pl.BlockSpec(memory_space=pl.ANY), vmem],
        out_specs=(pl.BlockSpec(memory_space=pl.ANY),) * 6,
        scratch_shapes=[
            pltpu.VMEM((local_rows, PIVOTS), f32),
            pltpu.VMEM(row_half.shape, bf16),
            pltpu.VMEM(row_half.shape, bf16),
            pltpu.VMEM(col_half.shape, bf16),
            pltpu.VMEM(col_half.shape, bf16),
            pltpu.VMEM(children.shape, f32),
            pltpu.VMEM((local_rows, TILE), f32),
            pltpu.VMEM((TILE, local_cols), f32),
            pltpu.VMEM((PIVOTS, PIVOTS), bf16),
            pltpu.VMEM((PIVOTS, PIVOTS), bf16),
            pltpu.VMEM((STEPS, TILE, local_cols), f32),
            pltpu.VMEM(slices, f32),
            pltpu.VMEM(slices, f32),
            pltpu.VMEM((2, 2, 4, 4, TILE, TILE), f32),
            pltpu.VMEM((PIVOTS, 2 * PIVOTS), f32),
            pltpu.VMEM((3 * TILE, (STEPS + 1) * TILE), bf16),
            pltpu.VMEM((3 * TILE, (STEPS + 1) * TILE), bf16),
            pltpu.SemaphoreType.DMA((2,)),
            pltpu.SemaphoreType.DMA((10,)),
            pltpu.SemaphoreType.DMA((4,)),
            pltpu.SemaphoreType.DMA((COPIES,)),
            pltpu.SemaphoreType.DMA((COPIES,)),
        ],
        compiler_params=pltpu.CompilerParams(
            vmem_limit_bytes=60 * MIB, collective_id=0, has_side_effects=True
        ),
        cost_estimate=pl.CostEstimate(flops=5 * 10**10, bytes_accessed=8 * MIB, transcendentals=0),
        name="gather_factor",
    )(child_map, front, children)


def update_kernel(slots_ref, front_ref, moved_ref, solved_ref, uh_ref, ul_ref, bh_ref, bl_ref, out_ref, lower_ref):
    step = pl.program_id(0)
    row = lax.broadcasted_iota(jnp.int32, solved_ref.shape, 0) + slots_ref[2, step] * TILE
    col = lax.broadcasted_iota(jnp.int32, solved_ref.shape, 1)
    lower_ref[...] = jnp.where(row >= col, solved_ref[...], 0.0)
    for n in range(front_ref.shape[0] // QUARTER):
        block = slice(n * QUARTER, (n + 1) * QUARTER)
        out_ref[block] = front_ref[block] - dot3(uh_ref[block], ul_ref[block], bh_ref[...], bl_ref[...], ((1,), (0,)))
    for child in range(2):
        for tile in range(6):
            slot = slots_ref[1, child * 6 + tile]

            @pl.when(slot // (QUARTER // TILE) == step)
            def _():
                col = pl.ds(pl.multiple_of(slot % (QUARTER // TILE) * TILE, TILE), TILE)
                for run in range(3):
                    row = pl.ds(pl.multiple_of(slots_ref[0, child * 3 + run] * TILE, TILE), TILE)
                    out_ref[row, col] += moved_ref[child, run * TILE : (run + 1) * TILE, tile * TILE : (tile + 1) * TILE]


def update(slots, front, moved, solved, uh, ul, bh, bl):
    rows, cols = front.shape
    rows_whole = pl.BlockSpec((rows, PIVOTS), lambda j: (0, 0), pipeline_mode=pl.Buffered(1))
    block = pl.BlockSpec((rows, QUARTER), lambda j: (0, j))
    cols_block = pl.BlockSpec((PIVOTS, QUARTER), lambda j: (0, j))
    lower_block = pl.BlockSpec((rows // (cols // QUARTER), PIVOTS), lambda j: (j, 0))
    return pl.pallas_call(
        update_kernel,
        grid=(cols // QUARTER,),
        out_shape=(jax.ShapeDtypeStruct(front.shape, f32), jax.ShapeDtypeStruct(solved.shape, f32)),
        in_specs=[
            pl.BlockSpec(memory_space=pltpu.SMEM),
            block,
            pl.BlockSpec(moved.shape, lambda j: (0, 0, 0), pipeline_mode=pl.Buffered(1)),
            lower_block,
            rows_whole,
            rows_whole,
            cols_block,
            cols_block,
        ],
        out_specs=(block, lower_block),
        compiler_params=pltpu.CompilerParams(vmem_limit_bytes=60 * MIB),
        name="update",
    )(slots, front, moved, solved, uh, ul, bh, bl)


def per_device(front, children, child_map):
    rows, cols = lax.axis_size("row"), lax.axis_size("col")
    row_index, col_index = lax.axis_index("row"), lax.axis_index("col")
    solved, uh, ul, bh, bl, moved = gather_and_factor(child_map, front, children)
    starts = child_map[:, ::RUN]
    row_slots = (starts + (row_index - starts) % rows) // rows
    col_slots = (starts + (col_index - starts) % cols) // cols
    col_slots = col_slots[:, :, None] + jnp.arange(RUN // cols)[None, None, :]
    slots = jnp.zeros((3, 12), jnp.int32).at[0, :6].set(row_slots.reshape(-1)).at[1].set(col_slots.reshape(-1))
    slots = slots.at[2].set(jnp.arange(12) * rows + row_index)
    return update(slots, front, moved, solved, uh, ul, bh, bl)


def solution(mesh):
    return jax.shard_map(
        per_device,
        mesh=mesh,
        in_specs=(P("row", "col"), P(None, "row", "col"), P()),
        out_specs=(P("row", "col"), P("row", None)),
        check_vma=False,
    )
```
